256 devices in a mesh: grp: 16 (over y_hi, z), uly: 4 (over x), blk: 4 (over y_lo, core).
Axes of the slice: x: 4, y: 4 (y_hi: 2, y_lo: 2; y = y_hi * 2 + y_lo), z: 8, core: 2. Of those that a mesh axis runs over, the one named last changes fastest.
Arguments:
- q_in: bfloat16 [16, 3072, 2560], P(None, ('grp', 'uly', 'blk')), may hold values from -80 to 80
- k_in: bfloat16 [16, 3072, 2560], P(None, ('grp', 'uly', 'blk')), may hold values from -80 to 80
- v_in: bfloat16 [16, 3072, 2560], P(None, ('grp', 'uly', 'blk')), may hold values from -6 to 6
- q_gain: float32 [2560], replicated, may hold values from 1 to 3
- k_gain: float32 [2560], replicated, may hold values from 1 to 3
- lengths: int32 [16], replicated, may hold values from 1 to 3072, 30720 in all
Outputs:
- attended: bfloat16 [16, 3072, 2560], P(None, ('grp', 'uly', 'blk'))
The draws below stay inside these ranges and needn't reach their ends.
All inputs are finite; a program needn't handle non-finite values.
Results may differ from the reference program's by a relative error of at most 0.012.
The reference program's roundings to bfloat16 on the way (of `q_norm`, `k_norm` and `weights`) count: a program that leaves them out, or rounds other values in their place, can miss the bound.
Values may be sent and summed in bfloat16 or wider, within the bound.
A program may use at most 128 MiB of HBM per device.

```python
import math
import jax
import jax.numpy as jnp
import numpy as np
from jax import lax

HEADS = 20
HD = 128
INNER = 2560
SEQ = 3072
NREQ = 16
TOTAL_LIVE = 30720
N_GRP = 16
N_ULY = 4
N_BLK = 4


def planted_pair(key, strength):
    key_q, key_k, key_a = jax.random.split(key, 3)
    queries = jnp.clip(jax.random.normal(key_q, (NREQ, SEQ, INNER), jnp.float32), -6.0, 6.0)
    keys = jnp.clip(jax.random.normal(key_k, (NREQ, SEQ, INNER), jnp.float32), -6.0, 6.0)
    factor = jax.random.uniform(key_a, (NREQ, SEQ, 1), jnp.float32, 6.0, 10.0)
    row = jnp.arange(SEQ, dtype=jnp.int32)[None, :, None]
    feature = jnp.arange(INNER, dtype=jnp.int32)[None, None, :]
    first_key = row % 97 == 6
    second_key = row % 97 == 7
    asking = row % 97 == 5
    copied = jnp.where(second_key, keys, keys)
    lift = jnp.where(first_key, factor, jnp.where(second_key, jnp.roll(factor, 1, axis=1) * 0.995, 1.0))
    lift = jnp.where(feature < HD, 1.0 + strength * (lift - 1.0), 1.0)
    keys_out = copied * lift
    queries_out = jnp.where(asking, queries, queries)
    return (queries_out, keys_out)


def draw_q_in(key, part):
    queries, keys = planted_pair(key, 0.0)
    return queries.astype(jnp.bfloat16)


def draw_k_in(key, part):
    queries, keys = planted_pair(key, 0.0)
    return keys.astype(jnp.bfloat16)


def block_scale(own_key, shape, cuts, least, largest):
    loudness = 1.0
    for axis_at, shards_of in cuts:
        heights = jax.random.uniform(jax.random.fold_in(jax.random.fold_in(own_key, 6), axis_at), (shards_of,), jnp.float32, least / len(cuts), largest / len(cuts))
        loudness = loudness * jnp.repeat(jnp.exp(heights), shape[axis_at] // shards_of).reshape((-1,) + (1,) * (len(shape) - 1 - axis_at))
    return loudness


def profile(amount, total, most, skew):
    weights = [(1 << 20) // math.isqrt(rank ** skew) + 1 for rank in range(2, amount + 1)]
    surplus, counts = total - most - (amount - 1), [1] * (amount - 1)
    while surplus > 0:
        free = [i for i in range(amount - 1) if counts[i] < most]
        whole, budget = sum([weights[i] for i in free]), surplus
        for i in free:
            addition = min(most - counts[i], max(1, budget * weights[i] // whole), surplus)
            counts[i] = counts[i] + addition
            surplus = surplus - addition
    return np.array([most] + counts)


def uneven(rng, amount, total, reach, skew):
    if amount == 2:
        one = jax.random.randint(rng, (), max(1, total - reach), min(reach, total - 1) + 1)
        return jnp.stack([one, total - one])
    sizes = jnp.asarray(profile(amount, total, reach, skew), jnp.int32)
    twos = (amount - 1) // 2
    source_of, receiver = sizes[1:1 + 2 * twos:2], sizes[2:2 + 2 * twos:2]
    slack = jnp.minimum(source_of - 1, reach - receiver)
    moved = jax.random.randint(jax.random.fold_in(rng, 1), (twos,), 0, 1 << 20) % (slack + 1)
    sizes = sizes.at[1:1 + 2 * twos:2].set(source_of - moved).at[2:2 + 2 * twos:2].set(receiver + moved)
    return sizes[jax.random.permutation(jax.random.fold_in(rng, 2), amount)]


def gaussian(stream_key, shape, scale, limit, pieces=(), held_as=jnp.bfloat16):
    result = scale * jax.random.normal(stream_key, shape, jnp.float32)
    if pieces:
        result = result * block_scale(stream_key, shape, pieces, -0.22, 0.18)
    return jnp.clip(result, -limit, limit).astype(held_as)


def setup_inputs(seed: int = 0) -> dict:
    seeds = jax.random.split(jax.random.key(seed), 7)
    q_in = draw_q_in(jax.random.fold_in(seeds[6], 71), 0)
    k_in = draw_k_in(jax.random.fold_in(seeds[6], 71), 0)
    v_in = gaussian(seeds[2], (NREQ, SEQ, INNER), 1.0, 6.0, ((1, 256),))
    q_gain = jnp.clip(jnp.exp(jax.random.uniform(seeds[3], (INNER,), jnp.float32, math.log(1.0), math.log(3.0))), 1.0, 3.0)
    k_gain = jnp.clip(jnp.exp(jax.random.uniform(seeds[4], (INNER,), jnp.float32, math.log(1.0), math.log(3.0))), 1.0, 3.0)
    lengths = uneven(seeds[5], NREQ, TOTAL_LIVE, SEQ, 2).astype(jnp.int32)
    return dict(q_in=q_in, k_in=k_in, v_in=v_in, q_gain=q_gain, k_gain=k_gain, lengths=lengths)


def slot_positions():
    index = jnp.arange(SEQ, dtype=jnp.int32)
    slice_rows = SEQ // (N_GRP * N_ULY * N_BLK)
    inner_row = index % slice_rows
    piece = index // slice_rows
    blk_part = piece % N_BLK
    uly_part = piece // N_BLK % N_ULY
    grp_part = piece // (N_BLK * N_ULY)
    return ((blk_part * N_ULY + uly_part) * N_GRP + grp_part) * slice_rows + inner_row

def rms_scale(values, gain):
    wide = values.astype(jnp.float32)
    power = lax.optimization_barrier(jnp.mean(wide * wide, axis=-1, keepdims=True))
    return (wide * lax.rsqrt(power + 1e-06) * gain).astype(jnp.bfloat16)

def reference(q_in, k_in, v_in, q_gain, k_gain, lengths):
    where_slot = slot_positions()

    def one_request(items):
        queries, keys, values, count = items
        live = where_slot < count
        q_norm = rms_scale(queries, q_gain).reshape(SEQ, HEADS, HD).transpose(1, 0, 2)
        k_norm = rms_scale(keys, k_gain).reshape(SEQ, HEADS, HD).transpose(1, 0, 2)
        v_heads = values.reshape(SEQ, HEADS, HD).transpose(1, 0, 2)

        def one_head(parts):
            q_head, k_head, v_head = parts
            scores = jnp.dot(q_head, k_head.T, preferred_element_type=jnp.float32) * HD ** (-0.5)
            scores = jnp.where(live[None, :], scores, -jnp.inf)
            top = lax.optimization_barrier(jnp.max(scores, axis=-1, keepdims=True))
            weights = jnp.where(live[None, :], jnp.exp(scores - top), jnp.float32(0.0))
            total = lax.optimization_barrier(jnp.sum(weights, axis=-1, keepdims=True))
            mixed = jnp.dot(weights.astype(jnp.bfloat16), v_head, preferred_element_type=jnp.float32)
            return mixed / total
        heads_out = lax.map(one_head, (q_norm, k_norm, v_heads))
        joined = heads_out.transpose(1, 0, 2).reshape(SEQ, INNER)
        return jnp.where(live[:, None], joined, jnp.float32(0.0)).astype(jnp.bfloat16)
    return lax.map(one_request, (q_in, k_in, v_in, lengths))
```

```python
import functools
import math

import jax
import jax.numpy as jnp
from jax import lax
from jax.experimental import pallas as pl
from jax.experimental.pallas import tpu as pltpu
from jax.sharding import PartitionSpec as P

HD = 128
T = 12
R = 16
HALF = 1280
SLOTS = 64
KEYS = 3072
TILE = 384
LOG2E = math.log2(math.e)
MESH = pl.DeviceIdType.MESH
BF = jnp.bfloat16
F32 = jnp.float32


def slot_pos(shape, slot, zpar):
    w = lax.broadcasted_iota(jnp.int32, shape, 1)
    cc = (w >= T).astype(jnp.int32)
    t = w - T * cc
    yl = slot & 1
    x = (slot >> 1) & 3
    zh = (slot >> 3) & 3
    yh = slot >> 5
    z = zh * 2 + zpar
    return ((((yl * 2 + cc) * 4 + x) * 2 + yh) * 8 + z) * T + t


def kernel(
    len_ref, q_ref, k_ref, v_ref, qg_ref, kg_ref, out_ref,
    halves, mates, perm, sb, ss, rb, rsh, rm, rmsh, ka, va, scr, prb, of,
    obs, oshs, ob, osh, fin,
    ex_s, ex_r, main_s, main_r, fwd_s, fwd_r, sh_s, sh_same, sh_other, fsh_s, fsh_r,
    o_s, o_r, osh_s, osh_r, fin_s, fin_r, fin_l,
):
    g = lax.axis_index("grp")
    x = lax.axis_index("uly")
    blk = lax.axis_index("blk")
    c = blk % 2
    yl = blk // 2
    z = g % 8
    yh = g // 8
    zp = z % 2
    zh = z // 2
    slot = ((yh * 4 + zh) * 4 + x) * 2 + yl
    sgrp = slot // 16
    xhalf = x // 2
    xl_me = x % 2
    count = len_ref[g]
    mate = (g, x, yl * 2 + 1 - c)
    own = jnp.logical_and(xhalf == c, zp == c)

    def dest(i):
        dr = i % 16
        xl = (i // 16) % 2
        dyl = i // 32
        r = ((yh + dr // 8) % 2) * 8 + (z + dr) % 8
        y2 = (yl + dyl) % 2
        return r, xl, y2, (r, 2 * c + xl, y2 * 2 + zp)

    def is_self(i):
        return jnp.logical_and(own, i == xl_me * 16)

    def source(s):
        return (
            (s // 32) * 8 + ((s // 8) % 4) * 2 + c,
            (s // 2) % 4,
            (s % 2) * 2 + xhalf,
        )

    def remote(src, dst, ssem, rsem, to):
        return pltpu.make_async_remote_copy(
            src_ref=src, dst_ref=dst, send_sem=ssem, recv_sem=rsem,
            device_id=to, device_id_type=MESH,
        )

    barrier = pltpu.get_barrier_semaphore()

    def greet(i, carry):
        me_too = is_self(i)
        to = dest(i)[3]

        @pl.when(jnp.logical_not(me_too))
        def _():
            pl.semaphore_signal(barrier, inc=1, device_id=to, device_id_type=MESH)

        @pl.when(jnp.logical_not(jnp.logical_and(own, i == slot)))
        def _():
            pl.semaphore_signal(barrier, inc=1, device_id=source(i), device_id_type=MESH)

        return carry

    lax.fori_loop(0, SLOTS, greet, 0)
    pl.semaphore_signal(barrier, inc=1, device_id=mate, device_id_type=MESH)

    def norm_into(ref, gain_ref, at):
        def one(t, carry):
            wide = ref[t].astype(F32)
            power = jnp.mean(wide * wide, axis=-1, keepdims=True)
            y = (wide * lax.rsqrt(power + 1e-06) * gain_ref[...]).astype(BF)
            halves[0, at, t] = y[:, :HALF]
            halves[1, at, t] = y[:, HALF:]
            return carry

        lax.fori_loop(0, T, one, 0)

    def move_v(t, carry):
        halves[0, 2, t] = v_ref[t, :, :HALF]
        halves[1, 2, t] = v_ref[t, :, HALF:]
        return carry

    norm_into(q_ref, qg_ref, 0)
    norm_into(k_ref, kg_ref, 1)
    lax.fori_loop(0, T, move_v, 0)

    @pl.when(own)
    def _():
        pl.semaphore_wait(barrier, 2 * SLOTS - 1)

    @pl.when(jnp.logical_not(own))
    def _():
        pl.semaphore_wait(barrier, 2 * SLOTS + 1)

    exch = []
    for at in range(3):
        cp = remote(halves.at[1 - c, at], mates.at[at], ex_s.at[at], ex_r.at[at], mate)
        cp.start()
        exch.append(cp)

    shape = (R * 2 * T, R * 2 * T)
    orow = lax.broadcasted_iota(jnp.int32, (R, 2 * T, R * 2 * T), 0)
    ow = lax.broadcasted_iota(jnp.int32, (R, 2 * T, R * 2 * T), 1)
    occ = (ow >= T).astype(jnp.int32)
    want = (jnp.where(occ == c, 0, 1) * T + ow - T * occ) * R + orow
    col = lax.broadcasted_iota(jnp.int32, (R, 2 * T, R * 2 * T), 2)
    perm[...] = (want == col).astype(F32).reshape(shape).astype(BF)

    lane0 = (lax.broadcasted_iota(jnp.int32, (TILE, HD), 1) == 0).astype(F32).astype(BF)

    def live_rows(first, step, offset, zpar):
        s = (lax.broadcasted_iota(jnp.int32, (16, 2 * T, HD), 0) + first) * step + offset
        return (slot_pos((16, 2 * T, HD), s, zpar) < count).astype(F32).reshape(TILE, HD)

    def masks(i, carry):
        half = i // 4
        flag = live_rows((i % 4) * 16, 1, 0, jnp.where(half == 0, c, 1 - c))
        rows = pl.ds(pl.multiple_of(i * TILE, TILE), TILE)
        for h in range(3):
            ka[h, rows, HD:] = ((flag - 1.0) * 1e30).astype(BF)
            va[h, rows, HD:] = jnp.ones((TILE, HD), BF)
        return carry

    lax.fori_loop(0, 8, masks, 0)

    for at in range(3):
        exch[at].wait()

    def pack(at, xl, first, width):
        cols = slice(xl * 640 + first * HD, xl * 640 + (first + width) * HD)
        mine = halves[c, at, :, :, cols].reshape(T * R, width * HD)
        theirs = mates[at, :, :, cols].reshape(T * R, width * HD)
        both = jnp.concatenate([mine, theirs], axis=0)
        res = jnp.dot(perm[...], both, preferred_element_type=F32)
        return res.reshape(R, 2 * T, width * HD)

    for at in range(3):
        for xl in range(2):
            for y2 in range(2):
                res = pack(at, xl, 3 * y2, 2)
                two = jnp.concatenate([res[:, :, :HD], res[:, :, HD:]], axis=1)
                sb[:, xl, y2, at * 48 : at * 48 + 48, :] = two.astype(BF)

    def send_main(i, carry):
        r, xl, y2, to = dest(i)
        src = sb.at[r, xl, y2]
        dst = rb.at[slot]

        @pl.when(is_self(i))
        def _():
            pltpu.make_async_copy(src, dst, main_r.at[sgrp]).start()

        @pl.when(jnp.logical_not(is_self(i)))
        def _():
            remote(src, dst, main_s, main_r.at[sgrp], to).start()

        return carry

    lax.fori_loop(0, SLOTS, send_main, 0)

    for xl in range(2):
        kv = jnp.concatenate([pack(1, xl, 2, 1), pack(2, xl, 2, 1)], axis=1)
        ss[:, xl, 0:48, :] = kv.astype(BF)
        qq = jnp.concatenate([pack(0, xl, 2, 1), jnp.zeros((R, 8, HD), F32)], axis=1)
        ss[:, xl, 48:80, :] = qq.astype(BF)

    def send_shared(i, carry):
        r, xl, y2, to = dest(i)

        @pl.when(i < 32)
        def _():
            src = ss.at[r, xl]
            dst = rsh.at[slot // 2, yl]

            @pl.when(is_self(i))
            def _():
                pltpu.make_async_copy(src, dst, sh_same.at[sgrp]).start()

            @pl.when(jnp.logical_not(is_self(i)))
            def _():
                remote(src, dst, sh_s.at[0], sh_same.at[sgrp], to).start()

        @pl.when(i >= 32)
        def _():
            src = ss.at[r, xl, pl.ds(0, 48)]
            dst = rsh.at[slot // 2, yl, pl.ds(0, 48)]
            remote(src, dst, sh_s.at[1], sh_other.at[sgrp], to).start()

        return carry

    lax.fori_loop(0, SLOTS, send_shared, 0)

    def place(ref, h, rows, value):
        ref[h, rows, :HD] = value.reshape(TILE, HD).astype(BF)

    def wait_for(ref, sem):
        pltpu.make_async_copy(ref, ref, sem).wait()

    forwards = []
    for i in range(4):
        at = pl.ds(16 * i, 16)
        wait_for(rb.at[at], main_r.at[i])
        cp = remote(
            rb.at[at, pl.ds(48, 96)], rm.at[at], fwd_s.at[i], fwd_r.at[i], mate
        )
        cp.start()
        forwards.append(cp)
        kk = rb[16 * i : 16 * i + 16, 48:96, :].astype(F32)
        vv = rb[16 * i : 16 * i + 16, 96:144, :].astype(F32)
        rows = slice(i * TILE, (i + 1) * TILE)
        for h in range(2):
            place(ka, h, rows, kk[:, 24 * h : 24 * h + 24])
            place(va, h, rows, vv[:, 24 * h : 24 * h + 24])
    for i in range(4):
        forwards[i].wait()
        kk = rm[16 * i : 16 * i + 16, 0:48, :].astype(F32)
        vv = rm[16 * i : 16 * i + 16, 48:96, :].astype(F32)
        rows = slice((i + 4) * TILE, (i + 5) * TILE)
        for h in range(2):
            place(ka, h, rows, kk[:, 24 * h : 24 * h + 24])
            place(va, h, rows, vv[:, 24 * h : 24 * h + 24])

    scale = F32(HD ** (-0.5) * LOG2E)

    def attend(q, h, live):
        qa = jnp.concatenate([q, lane0], axis=1)
        top = None
        step = 512
        for j in range(KEYS // step):
            cols = slice(j * step, (j + 1) * step)
            part = lax.dot_general(
                qa, ka[h, cols, :], (((1,), (1,)), ((), ())),
                preferred_element_type=F32,
            )
            scr[:, cols] = part
            for i in range(step // HD):
                piece = part[:, i * HD : (i + 1) * HD]
                top = piece if top is None else jnp.maximum(top, piece)
        peak = jnp.max(top, axis=1, keepdims=True)
        for j in range(KEYS // step):
            cols = slice(j * step, (j + 1) * step)
            prb[:, cols] = jnp.exp2((scr[:, cols] - peak) * scale).astype(BF)
        mixed = jnp.dot(prb[...], va[h], preferred_element_type=F32)
        return jnp.where(live > 0.0, mixed[:, :HD] / mixed[:, HD:], 0.0)

    def main_tile(i, carry):
        at = pl.ds(pl.multiple_of(i * 16, 16), 16)
        live = live_rows(i * 16, 1, 0, c)
        qq = rb[at, 0:48, :].astype(F32)
        res = []
        for h in range(2):
            q = qq[:, 24 * h : 24 * h + 24].reshape(TILE, HD).astype(BF)
            res.append(attend(q, h, live).reshape(16, 2 * T, HD))
        obs[at] = jnp.concatenate(res, axis=1).astype(BF)

        def send(j, carry):
            s = i * 16 + j
            dst = ob.at[g, xl_me, yl]
            mine = jnp.logical_and(own, s == slot)

            @pl.when(mine)
            def _():
                pltpu.make_async_copy(obs.at[s], dst, o_r.at[xl_me]).start()

            @pl.when(jnp.logical_not(mine))
            def _():
                remote(obs.at[s], dst, o_s, o_r.at[xl_me], source(s)).start()

            return carry

        lax.fori_loop(0, 16, send, 0)
        return carry

    lax.fori_loop(0, 4, main_tile, 0)

    forwards = []
    for i in range(4):
        at = pl.ds(8 * i, 8)
        wait_for(rsh.at[at, yl], sh_same.at[i])
        wait_for(rsh.at[at, 1 - yl, pl.ds(0, 48)], sh_other.at[i])
        cp = remote(
            rsh.at[at, :, pl.ds(0, 48)], rmsh.at[at], fsh_s.at[i], fsh_r.at[i], mate
        )
        cp.start()
        forwards.append(cp)
        kv = rsh[8 * i : 8 * i + 8, :, 0:48, :].astype(F32).reshape(16, 48, HD)
        rows = slice(i * TILE, (i + 1) * TILE)
        place(ka, 2, rows, kv[:, 0:24])
        place(va, 2, rows, kv[:, 24:48])
    for i in range(4):
        forwards[i].wait()
        kv = rmsh[8 * i : 8 * i + 8].astype(F32).reshape(16, 48, HD)
        rows = slice((i + 4) * TILE, (i + 5) * TILE)
        place(ka, 2, rows, kv[:, 0:24])
        place(va, 2, rows, kv[:, 24:48])

    def shared_tile(i, carry):
        at = pl.ds(pl.multiple_of(i * 16, 16), 16)
        live = live_rows(i * 16, 2, yl, c)
        qq = rsh[at, yl, 48:80, :].astype(F32)
        q = qq[:, 0:24].reshape(TILE, HD).astype(BF)
        res = attend(q, 2, live).reshape(16, 2 * T, HD)
        oshs[at] = jnp.concatenate([res, jnp.zeros((16, 8, HD), F32)], axis=1).astype(BF)

        def send(j, carry):
            m = i * 16 + j
            s = m * 2 + yl
            dst = osh.at[g, xl_me]
            mine = jnp.logical_and(own, s == slot)

            @pl.when(mine)
            def _():
                pltpu.make_async_copy(oshs.at[m], dst, osh_r.at[xl_me]).start()

            @pl.when(jnp.logical_not(mine))
            def _():
                remote(oshs.at[m], dst, osh_s, osh_r.at[xl_me], source(s)).start()

            return carry

        lax.fori_loop(0, 16, send, 0)
        return carry

    lax.fori_loop(0, 2, shared_tile, 0)

    def unpack(value):
        res = lax.dot_general(
            perm[...], value, (((0,), (0,)), ((), ())), preferred_element_type=F32
        )
        return res.astype(BF)

    def store(res, xl, first, width):
        cols = slice(xl * 640 + first * HD, xl * 640 + (first + width) * HD)
        fin[0, :, :, cols] = res[: T * R].reshape(T, R, width * HD)
        fin[1, :, :, cols] = res[T * R :].reshape(T, R, width * HD)

    for xl in range(2):
        wait_for(ob.at[:, xl], o_r.at[xl])
        for y2 in range(2):
            got = ob[:, xl, y2].astype(F32)
            flat = [got[:, 24 * h : 24 * h + 24].reshape(TILE, HD) for h in range(2)]
            store(unpack(jnp.concatenate(flat, axis=1).astype(BF)), xl, 3 * y2, 2)
    for xl in range(2):
        wait_for(osh.at[:, xl], osh_r.at[xl])
        got = osh[:, xl].astype(F32)[:, 0:24].reshape(TILE, HD)
        store(unpack(got.astype(BF)), xl, 2, 1)

    cols = pl.ds(pl.multiple_of(c * HALF, HALF), HALF)
    far = remote(fin.at[1], out_ref.at[:, :, cols], fin_s, fin_r, mate)
    far.start()
    near = pltpu.make_async_copy(fin.at[0], out_ref.at[:, :, cols], fin_l)
    near.start()
    far.wait()
    near.wait()

    @pl.when(own)
    def _():
        wait_for(rb.at[pl.ds(0, SLOTS - 1)], main_s)
        wait_for(rsh.at[pl.ds(0, 31), 0], sh_s.at[0])
        wait_for(obs.at[pl.ds(0, SLOTS - 1)], o_s)
        wait_for(oshs.at[pl.ds(0, 31)], osh_s)

    @pl.when(jnp.logical_not(own))
    def _():
        wait_for(rb, main_s)
        wait_for(rsh.at[:, 0], sh_s.at[0])
        wait_for(obs, o_s)
        wait_for(oshs, osh_s)

    wait_for(rsh.at[:, 0, pl.ds(0, 48)], sh_s.at[1])


def per_device(q_in, k_in, v_in, q_gain, k_gain, lengths):
    vm = pl.BlockSpec(memory_space=pltpu.VMEM)
    dma = pltpu.SemaphoreType.DMA
    scratch = [
        pltpu.VMEM((2, 3, T, R, HALF), BF),
        pltpu.VMEM((3, T, R, HALF), BF),
        pltpu.VMEM((TILE, TILE), BF),
        pltpu.VMEM((R, 2, 2, 144, HD), BF),
        pltpu.VMEM((R, 2, 80, HD), BF),
        pltpu.VMEM((SLOTS, 144, HD), BF),
        pltpu.VMEM((SLOTS // 2, 2, 80, HD), BF),
        pltpu.VMEM((SLOTS, 96, HD), BF),
        pltpu.VMEM((SLOTS // 2, 2, 48, HD), BF),
        pltpu.VMEM((3, KEYS, 2 * HD), BF),
        pltpu.VMEM((3, KEYS, 2 * HD), BF),
        pltpu.VMEM((TILE, KEYS), F32),
        pltpu.VMEM((TILE, KEYS), BF),
        pltpu.VMEM((8, HD), F32),
        pltpu.VMEM((SLOTS, 48, HD), BF),
        pltpu.VMEM((SLOTS // 2, 32, HD), BF),
        pltpu.VMEM((R, 2, 2, 48, HD), BF),
        pltpu.VMEM((R, 2, 32, HD), BF),
        pltpu.VMEM((2, T, R, HALF), BF),
        dma((3,)), dma((3,)),
        dma, dma((4,)),
        dma((4,)), dma((4,)),
        dma((2,)), dma((4,)), dma((4,)),
        dma((4,)), dma((4,)),
        dma, dma((2,)),
        dma, dma((2,)),
        dma, dma, dma,
    ]
    res = pl.pallas_call(
        kernel,
        out_shape=jax.ShapeDtypeStruct((T, R, 2 * HALF), BF),
        in_specs=[pl.BlockSpec(memory_space=pltpu.SMEM), vm, vm, vm, vm, vm],
        out_specs=pl.BlockSpec(memory_space=pl.ANY),
        scratch_shapes=scratch,
        compiler_params=pltpu.CompilerParams(
            collective_id=0, has_side_effects=True, vmem_limit_bytes=60 << 20
        ),
        name="attend",
    )(
        lengths,
        jnp.transpose(q_in, (1, 0, 2)),
        jnp.transpose(k_in, (1, 0, 2)),
        jnp.transpose(v_in, (1, 0, 2)),
        q_gain[None, :],
        k_gain[None, :],
    )
    return jnp.transpose(res, (1, 0, 2))


def solution(mesh):
    placed = P(None, ("grp", "uly", "blk"), None)
    return jax.shard_map(
        per_device,
        mesh=mesh,
        in_specs=(placed, placed, placed, P(), P(), P()),
        out_specs=placed,
        check_vma=False,
    )
```

```python
import functools
import math

import jax
import jax.numpy as jnp
from jax import lax
from jax.experimental import pallas as pl
from jax.experimental.pallas import tpu as pltpu
from jax.sharding import PartitionSpec as P

HD = 128
T = 12
R = 16
HALF = 1280
SLOTS = 64
KEYS = 3072
TILE = 384
LOG2E = math.log2(math.e)
MESH = pl.DeviceIdType.MESH
BF = jnp.bfloat16
F32 = jnp.float32


def slot_pos(shape, slot, zpar):
    w = lax.broadcasted_iota(jnp.int32, shape, 1)
    cc = (w >= T).astype(jnp.int32)
    t = w - T * cc
    yl = slot & 1
    x = (slot >> 1) & 3
    zh = (slot >> 3) & 3
    yh = slot >> 5
    z = zh * 2 + zpar
    return ((((yl * 2 + cc) * 4 + x) * 2 + yh) * 8 + z) * T + t


def kernel(
    len_ref, q_ref, k_ref, v_ref, qg_ref, kg_ref, out_ref,
    halves, mates, perm, sb, ss, rb, rsh, rn, rm, rmsh, ka, va, scr, prb,
    obs, oshs, ob, osh, fin,
    ex_s, ex_r, main_s, main_r, fwd_s, fwd_r, sh_s, sh_r, near_s, near_r, fsh_s, fsh_r,
    o_s, o_r, osh_s, osh_r, fin_s, fin_r, fin_l,
):
    g = lax.axis_index("grp")
    x = lax.axis_index("uly")
    blk = lax.axis_index("blk")
    c = blk % 2
    yl = blk // 2
    z = g % 8
    yh = g // 8
    zp = z % 2
    zh = z // 2
    slot = ((yh * 4 + zh) * 4 + x) * 2 + yl
    sgrp = slot // 16
    xhalf = x // 2
    xl_me = x % 2
    count = len_ref[g]
    mate = (g, x, yl * 2 + 1 - c)
    next_chip = (g, x, (1 - yl) * 2 + c)
    own = jnp.logical_and(xhalf == c, zp == c)

    def dest(i):
        dr = i % 16
        xl = (i // 16) % 2
        dyl = i // 32
        r = ((yh + dr // 8) % 2) * 8 + (z + dr) % 8
        y2 = (yl + dyl) % 2
        return r, xl, y2, (r, 2 * c + xl, y2 * 2 + zp)

    def is_self(i):
        return jnp.logical_and(own, i == xl_me * 16)

    def source(s):
        return (
            (s // 32) * 8 + ((s // 8) % 4) * 2 + c,
            (s // 2) % 4,
            (s % 2) * 2 + xhalf,
        )

    def remote(src, dst, ssem, rsem, to):
        return pltpu.make_async_remote_copy(
            src_ref=src, dst_ref=dst, send_sem=ssem, recv_sem=rsem,
            device_id=to, device_id_type=MESH,
        )

    barrier = pltpu.get_barrier_semaphore()

    def greet(i, carry):
        me_too = is_self(i)
        to = dest(i)[3]

        @pl.when(jnp.logical_not(me_too))
        def _():
            pl.semaphore_signal(barrier, inc=1, device_id=to, device_id_type=MESH)

        @pl.when(jnp.logical_not(jnp.logical_and(own, i == slot)))
        def _():
            pl.semaphore_signal(barrier, inc=1, device_id=source(i), device_id_type=MESH)

        return carry

    lax.fori_loop(0, SLOTS, greet, 0)
    pl.semaphore_signal(barrier, inc=1, device_id=mate, device_id_type=MESH)
    pl.semaphore_signal(barrier, inc=1, device_id=next_chip, device_id_type=MESH)

    def norm_into(ref, gain_ref, at):
        def one(t, carry):
            wide = ref[t].astype(F32)
            power = jnp.mean(wide * wide, axis=-1, keepdims=True)
            y = (wide * lax.rsqrt(power + 1e-06) * gain_ref[...][None, :]).astype(BF)
            halves[0, at, t] = y[:, :HALF]
            halves[1, at, t] = y[:, HALF:]
            return carry

        lax.fori_loop(0, T, one, 0)

    def move_v(t, carry):
        halves[0, 2, t] = v_ref[t, :, :HALF]
        halves[1, 2, t] = v_ref[t, :, HALF:]
        return carry

    norm_into(q_ref, qg_ref, 0)
    norm_into(k_ref, kg_ref, 1)
    lax.fori_loop(0, T, move_v, 0)

    @pl.when(own)
    def _():
        pl.semaphore_wait(barrier, 2 * SLOTS)

    @pl.when(jnp.logical_not(own))
    def _():
        pl.semaphore_wait(barrier, 2 * SLOTS + 2)

    exch = []
    for at in range(3):
        cp = remote(halves.at[1 - c, at], mates.at[at], ex_s.at[at], ex_r.at[at], mate)
        cp.start()
        exch.append(cp)

    shape = (R * 2 * T, R * 2 * T)
    orow = lax.broadcasted_iota(jnp.int32, (R, 2 * T, R * 2 * T), 0)
    ow = lax.broadcasted_iota(jnp.int32, (R, 2 * T, R * 2 * T), 1)
    occ = (ow >= T).astype(jnp.int32)
    want = (jnp.where(occ == c, 0, 1) * T + ow - T * occ) * R + orow
    col = lax.broadcasted_iota(jnp.int32, (R, 2 * T, R * 2 * T), 2)
    perm[...] = (want == col).astype(F32).reshape(shape).astype(BF)

    lane0 = (lax.broadcasted_iota(jnp.int32, (TILE, HD), 1) == 0).astype(F32).astype(BF)

    def live_rows(first, step, offset, zpar):
        s = (lax.broadcasted_iota(jnp.int32, (16, 2 * T, HD), 0) + first) * step + offset
        return (slot_pos((16, 2 * T, HD), s, zpar) < count).astype(F32).reshape(TILE, HD)

    def masks(i, carry):
        half = i // 4
        flag = live_rows((i % 4) * 16, 1, 0, jnp.where(half == 0, c, 1 - c))
        rows = pl.ds(pl.multiple_of(i * TILE, TILE), TILE)
        for h in range(2):
            ka[h, rows, HD:] = ((flag - 1.0) * 1e30).astype(BF)
            va[h, rows, HD:] = jnp.ones((TILE, HD), BF)
        side = (i // 2) % 2
        flag = live_rows(
            (i % 2) * 16, 2, jnp.where(side == 0, yl, 1 - yl), jnp.where(half == 0, c, 1 - c)
        )
        ka[2, rows, HD:] = ((flag - 1.0) * 1e30).astype(BF)
        va[2, rows, HD:] = jnp.ones((TILE, HD), BF)
        return carry

    lax.fori_loop(0, 8, masks, 0)

    for at in range(3):
        exch[at].wait()

    def pack(at, xl, first, width):
        cols = slice(xl * 640 + first * HD, xl * 640 + (first + width) * HD)
        mine = halves[c, at, :, :, cols].reshape(T * R, width * HD)
        theirs = mates[at, :, :, cols].reshape(T * R, width * HD)
        both = jnp.concatenate([mine, theirs], axis=0)
        res = jnp.dot(perm[...], both, preferred_element_type=F32)
        return res.reshape(R, 2 * T, width * HD)

    for at in range(3):
        for xl in range(2):
            for y2 in range(2):
                res = pack(at, xl, 3 * y2, 2)
                two = jnp.concatenate([res[:, :, :HD], res[:, :, HD:]], axis=1)
                sb[:, xl, y2, at * 48 : at * 48 + 48, :] = two.astype(BF)

    def send_main(i, carry):
        r, xl, y2, to = dest(i)
        src = sb.at[r, xl, y2]
        dst = rb.at[slot]

        @pl.when(is_self(i))
        def _():
            pltpu.make_async_copy(src, dst, main_r.at[sgrp]).start()

        @pl.when(jnp.logical_not(is_self(i)))
        def _():
            remote(src, dst, main_s, main_r.at[sgrp], to).start()

        return carry

    lax.fori_loop(0, SLOTS, send_main, 0)

    for xl in range(2):
        kv = jnp.concatenate([pack(1, xl, 2, 1), pack(2, xl, 2, 1)], axis=1)
        ss[:, xl, 0:48, :] = kv.astype(BF)
        qq = jnp.concatenate([pack(0, xl, 2, 1), jnp.zeros((R, 8, HD), F32)], axis=1)
        ss[:, xl, 48:80, :] = qq.astype(BF)

    def send_shared(i, carry):
        r, xl, y2, to = dest(i)
        src = ss.at[r, xl]
        dst = rsh.at[slot // 2]

        @pl.when(is_self(i))
        def _():
            pltpu.make_async_copy(src, dst, sh_r.at[yh]).start()

        @pl.when(jnp.logical_not(is_self(i)))
        def _():
            remote(src, dst, sh_s, sh_r.at[yh], to).start()

        return carry

    lax.fori_loop(0, SLOTS // 2, send_shared, 0)

    def place(ref, h, rows, value):
        ref[h, rows, :HD] = value.reshape(TILE, HD).astype(BF)

    def wait_for(ref, sem):
        pltpu.make_async_copy(ref, ref, sem).wait()

    forwards = []
    for i in range(4):
        at = pl.ds(16 * i, 16)
        wait_for(rb.at[at], main_r.at[i])
        cp = remote(
            rb.at[at, pl.ds(48, 96)], rm.at[at], fwd_s.at[i], fwd_r.at[i], mate
        )
        cp.start()
        forwards.append(cp)
        kk = rb[16 * i : 16 * i + 16, 48:96, :].astype(F32)
        vv = rb[16 * i : 16 * i + 16, 96:144, :].astype(F32)
        rows = slice(i * TILE, (i + 1) * TILE)
        for h in range(2):
            place(ka, h, rows, kk[:, 24 * h : 24 * h + 24])
            place(va, h, rows, vv[:, 24 * h : 24 * h + 24])
    for i in range(4):
        forwards[i].wait()
        kk = rm[16 * i : 16 * i + 16, 0:48, :].astype(F32)
        vv = rm[16 * i : 16 * i + 16, 48:96, :].astype(F32)
        rows = slice((i + 4) * TILE, (i + 5) * TILE)
        for h in range(2):
            place(ka, h, rows, kk[:, 24 * h : 24 * h + 24])
            place(va, h, rows, vv[:, 24 * h : 24 * h + 24])

    scale = F32(HD ** (-0.5) * LOG2E)

    def attend(q, h, live):
        qa = jnp.concatenate([q, lane0], axis=1)
        top = None
        step = 512
        for j in range(KEYS // step):
            cols = slice(j * step, (j + 1) * step)
            part = lax.dot_general(
                qa, ka[h, cols, :], (((1,), (1,)), ((), ())),
                preferred_element_type=F32,
            )
            scr[:, cols] = part
            for i in range(step // HD):
                piece = part[:, i * HD : (i + 1) * HD]
                top = piece if top is None else jnp.maximum(top, piece)
        peak = jnp.max(top, axis=1, keepdims=True)
        for j in range(KEYS // step):
            cols = slice(j * step, (j + 1) * step)
            prb[:, cols] = jnp.exp2((scr[:, cols] - peak) * scale).astype(BF)
        mixed = jnp.dot(prb[...], va[h], preferred_element_type=F32)
        return jnp.where(live > 0.0, mixed[:, :HD] / mixed[:, HD:], 0.0)

    def main_tile(i, carry):
        at = pl.ds(pl.multiple_of(i * 16, 16), 16)
        live = live_rows(i * 16, 1, 0, c)
        qq = rb[at, 0:48, :].astype(F32)
        res = []
        for h in range(2):
            q = qq[:, 24 * h : 24 * h + 24].reshape(TILE, HD).astype(BF)
            res.append(attend(q, h, live).reshape(16, 2 * T, HD))
        obs[at] = jnp.concatenate(res, axis=1).astype(BF)

        def send(j, carry):
            s = i * 16 + j
            dst = ob.at[g, xl_me, yl]
            mine = jnp.logical_and(own, s == slot)

            @pl.when(mine)
            def _():
                pltpu.make_async_copy(obs.at[s], dst, o_r.at[xl_me]).start()

            @pl.when(jnp.logical_not(mine))
            def _():
                remote(obs.at[s], dst, o_s, o_r.at[xl_me], source(s)).start()

            return carry

        lax.fori_loop(0, 16, send, 0)
        return carry

    lax.fori_loop(0, 4, main_tile, 0)

    def place_shared(i, value):
        kv = value.astype(F32)
        rows = slice(i * TILE, (i + 1) * TILE)
        place(ka, 2, rows, kv[:, 0:24])
        place(va, 2, rows, kv[:, 24:48])

    across, along = [], []
    for i in range(2):
        at = pl.ds(16 * i, 16)
        part = rsh.at[at, pl.ds(0, 48)]
        wait_for(rsh.at[at], sh_r.at[i])
        across.append(remote(part, rn.at[at], near_s.at[i], near_r.at[i], next_chip))
        across[i].start()
        along.append(remote(part, rmsh.at[0, at], fsh_s.at[i], fsh_r.at[i], mate))
        along[i].start()
        place_shared(i, rsh[16 * i : 16 * i + 16, 0:48, :])
    for i in range(2):
        at = pl.ds(16 * i, 16)
        across[i].wait()
        along.append(
            remote(rn.at[at], rmsh.at[1, at], fsh_s.at[2 + i], fsh_r.at[2 + i], mate)
        )
        along[2 + i].start()
        place_shared(2 + i, rn[16 * i : 16 * i + 16])
    for i in range(4):
        along[i].wait()
        place_shared(4 + i, rmsh[i // 2, 16 * (i % 2) : 16 * (i % 2) + 16])

    def shared_tile(i, carry):
        at = pl.ds(pl.multiple_of(i * 16, 16), 16)
        live = live_rows(i * 16, 2, yl, c)
        qq = rsh[at, 48:80, :].astype(F32)
        q = qq[:, 0:24].reshape(TILE, HD).astype(BF)
        res = attend(q, 2, live).reshape(16, 2 * T, HD)
        oshs[at] = jnp.concatenate([res, jnp.zeros((16, 8, HD), F32)], axis=1).astype(BF)

        def send(j, carry):
            m = i * 16 + j
            s = m * 2 + yl
            dst = osh.at[g, xl_me]
            mine = jnp.logical_and(own, s == slot)

            @pl.when(mine)
            def _():
                pltpu.make_async_copy(oshs.at[m], dst, osh_r.at[xl_me]).start()

            @pl.when(jnp.logical_not(mine))
            def _():
                remote(oshs.at[m], dst, osh_s, osh_r.at[xl_me], source(s)).start()

            return carry

        lax.fori_loop(0, 16, send, 0)
        return carry

    lax.fori_loop(0, 2, shared_tile, 0)

    def unpack(value):
        res = lax.dot_general(
            perm[...], value, (((0,), (0,)), ((), ())), preferred_element_type=F32
        )
        return res.astype(BF)

    def store(res, xl, first, width):
        cols = slice(xl * 640 + first * HD, xl * 640 + (first + width) * HD)
        fin[0, :, :, cols] = res[: T * R].reshape(T, R, width * HD)
        fin[1, :, :, cols] = res[T * R :].reshape(T, R, width * HD)

    for xl in range(2):
        wait_for(ob.at[:, xl], o_r.at[xl])
        for y2 in range(2):
            got = ob[:, xl, y2].astype(F32)
            flat = [got[:, 24 * h : 24 * h + 24].reshape(TILE, HD) for h in range(2)]
            store(unpack(jnp.concatenate(flat, axis=1).astype(BF)), xl, 3 * y2, 2)
    for xl in range(2):
        wait_for(osh.at[:, xl], osh_r.at[xl])
        got = osh[:, xl].astype(F32)[:, 0:24].reshape(TILE, HD)
        store(unpack(got.astype(BF)), xl, 2, 1)

    cols = pl.ds(pl.multiple_of(c * HALF, HALF), HALF)
    far = remote(fin.at[1], out_ref.at[:, :, cols], fin_s, fin_r, mate)
    far.start()
    near = pltpu.make_async_copy(fin.at[0], out_ref.at[:, :, cols], fin_l)
    near.start()
    far.wait()
    near.wait()

    @pl.when(own)
    def _():
        wait_for(rb.at[pl.ds(0, SLOTS - 1)], main_s)
        wait_for(rsh.at[pl.ds(0, 31)], sh_s)
        wait_for(obs.at[pl.ds(0, SLOTS - 1)], o_s)
        wait_for(oshs.at[pl.ds(0, 31)], osh_s)

    @pl.when(jnp.logical_not(own))
    def _():
        wait_for(rb, main_s)
        wait_for(rsh, sh_s)
        wait_for(obs, o_s)
        wait_for(oshs, osh_s)


def per_device(q_in, k_in, v_in, q_gain, k_gain, lengths):
    vm = pl.BlockSpec(memory_space=pltpu.VMEM)
    dma = pltpu.SemaphoreType.DMA
    scratch = [
        pltpu.VMEM((2, 3, T, R, HALF), BF),
        pltpu.VMEM((3, T, R, HALF), BF),
        pltpu.VMEM((TILE, TILE), BF),
        pltpu.VMEM((R, 2, 2, 144, HD), BF),
        pltpu.VMEM((R, 2, 80, HD), BF),
        pltpu.VMEM((SLOTS, 144, HD), BF),
        pltpu.VMEM((SLOTS // 2, 80, HD), BF),
        pltpu.VMEM((SLOTS // 2, 48, HD), BF),
        pltpu.VMEM((SLOTS, 96, HD), BF),
        pltpu.VMEM((2, SLOTS // 2, 48, HD), BF),
        pltpu.VMEM((3, KEYS, 2 * HD), BF),
        pltpu.VMEM((3, KEYS, 2 * HD), BF),
        pltpu.VMEM((TILE, KEYS), F32),
        pltpu.VMEM((TILE, KEYS), BF),
        pltpu.VMEM((SLOTS, 48, HD), BF),
        pltpu.VMEM((SLOTS // 2, 32, HD), BF),
        pltpu.VMEM((R, 2, 2, 48, HD), BF),
        pltpu.VMEM((R, 2, 32, HD), BF),
        pltpu.VMEM((2, T, R, HALF), BF),
        dma((3,)), dma((3,)),
        dma, dma((4,)),
        dma((4,)), dma((4,)),
        dma, dma((2,)),
        dma((2,)), dma((2,)),
        dma((4,)), dma((4,)),
        dma, dma((2,)),
        dma, dma((2,)),
        dma, dma, dma,
    ]
    res = pl.pallas_call(
        kernel,
        out_shape=jax.ShapeDtypeStruct((T, R, 2 * HALF), BF),
        in_specs=[pl.BlockSpec(memory_space=pltpu.SMEM), vm, vm, vm, vm, vm],
        out_specs=pl.BlockSpec(memory_space=pl.ANY),
        scratch_shapes=scratch,
        compiler_params=pltpu.CompilerParams(
            collective_id=0, has_side_effects=True, vmem_limit_bytes=60 << 20
        ),
        name="attend",
    )(
        lengths,
        jnp.transpose(q_in, (1, 0, 2)),
        jnp.transpose(k_in, (1, 0, 2)),
        jnp.transpose(v_in, (1, 0, 2)),
        q_gain,
        k_gain,
    )
    return jnp.transpose(res, (1, 0, 2))


def solution(mesh):
    placed = P(None, ("grp", "uly", "blk"), None)
    return jax.shard_map(
        per_device,
        mesh=mesh,
        in_specs=(placed, placed, placed, P(), P(), P()),
        out_specs=placed,
        check_vma=False,
    )
```

```python
import functools
import math

import jax
import jax.numpy as jnp
from jax import lax
from jax.experimental import pallas as pl
from jax.experimental.pallas import tpu as pltpu
from jax.sharding import PartitionSpec as P

HD = 128
T = 12
R = 16
HALF = 1280
SLOTS = 64
KEYS = 3072
TILE = 384
BLOCK = 768
SUB = 256
REACH = 1536
CUT = 12
LOG2E = math.log2(math.e)
MESH = pl.DeviceIdType.MESH
BF = jnp.bfloat16
F32 = jnp.float32


def slot_pos(shape, slot, zpar):
    w = lax.broadcasted_iota(jnp.int32, shape, 1)
    cc = (w >= T).astype(jnp.int32)
    t = w - T * cc
    x = slot & 3
    zh = (slot >> 2) & 3
    yh = (slot >> 4) & 1
    yl = slot >> 5
    z = zh * 2 + zpar
    return ((((yl * 2 + cc) * 4 + x) * 2 + yh) * 8 + z) * T + t


def group_rank(yh, z):
    k = (z >> 1) + 4 * (z & 1)
    return jnp.where((k & 1) == yh, k, 15 - k)


def rank_group(k):
    j = k if k < 8 else 15 - k
    z = 2 * (j & 3) + (j >> 2)
    yh = (j & 1) if k < 8 else 1 - (j & 1)
    return yh * 8 + z


def kernel(
    cut,
    len_ref, q_ref, k_ref, v_ref, qg_ref, kg_ref, out_ref,
    halves, mates, perm, sb, ss, rel, rels, rb, rsh, rm, rmsh, ka, va, scr,
    obs, oshs, ob, osh, fin,
    ex_s, ex_r, main_s, main_r, fwd_s, fwd_r, sh_s, sh_r, fsh_s, fsh_r,
    rel_s, rel_r, rels_s, rels_r, o_s, o_r, osh_s, osh_r, fin_s, fin_r, fin_l,
):
    g = lax.axis_index("grp")
    x = lax.axis_index("uly")
    blk = lax.axis_index("blk")
    c = blk & 1
    yl = blk >> 1
    z = g & 7
    yh = g >> 3
    zp = z & 1
    zh = z >> 1
    slot = ((yl * 2 + yh) * 4 + zh) * 4 + x
    sgrp = slot >> 4
    xhalf = x >> 1
    xl_me = x & 1
    rank_me = group_rank(yh, z)
    short = rank_me >= cut
    three = yl == (zp ^ xl_me)
    mate = (g, x, yl * 2 + 1 - c)
    next_chip = (g, x, (1 - yl) * 2 + c)
    own = jnp.logical_and(xhalf == c, zp == c)

    def dest(i):
        dr = i & 15
        xl = (i >> 4) & 1
        ty = yh ^ (dr >> 3)
        tz = (z + dr) & 7
        y2 = yl ^ (i >> 5)
        return group_rank(ty, tz), xl, y2, ((ty << 3) | tz, 2 * c + xl, y2 * 2 + zp)

    def is_self(i):
        return jnp.logical_and(own, i == xl_me * 16)

    def source(s):
        return (
            (((s >> 4) & 1) << 3) | (((s >> 2) & 3) << 1) | c,
            s & 3,
            ((s >> 5) << 1) | xhalf,
        )

    def remote(src, dst, ssem, rsem, to):
        return pltpu.make_async_remote_copy(
            src_ref=src, dst_ref=dst, send_sem=ssem, recv_sem=rsem,
            device_id=to, device_id_type=MESH,
        )

    def send(src, dst, ssem, rsem, to, here):
        @pl.when(here)
        def _():
            pltpu.make_async_copy(src, dst, rsem).start()

        @pl.when(jnp.logical_not(here))
        def _():
            remote(src, dst, ssem, rsem, to).start()

    def wait_for(ref, sem):
        pltpu.make_async_copy(ref, ref, sem).wait()

    barrier = pltpu.get_barrier_semaphore()

    def greet(i, carry):
        @pl.when(jnp.logical_not(is_self(i)))
        def _():
            pl.semaphore_signal(barrier, inc=1, device_id=dest(i)[3], device_id_type=MESH)

        @pl.when(jnp.logical_not(jnp.logical_and(own, i == slot)))
        def _():
            pl.semaphore_signal(barrier, inc=1, device_id=source(i), device_id_type=MESH)

        return carry

    lax.fori_loop(0, SLOTS, greet, 0)
    pl.semaphore_signal(barrier, inc=1, device_id=mate, device_id_type=MESH)
    pl.semaphore_signal(barrier, inc=1, device_id=next_chip, device_id_type=MESH)

    sizes = [len_ref[i] for i in range(R)]
    ranks = []
    count = jnp.int32(0)
    for i in range(R):
        rank = jnp.int32(0)
        for j in range(R):
            if j != i:
                ahead = sizes[j] >= sizes[i] if j < i else sizes[j] > sizes[i]
                rank = rank + ahead.astype(jnp.int32)
        ranks.append(rank)
        count = count + jnp.where(rank == rank_me, sizes[i], 0)

    def norm_into(ref, gain_ref, at):
        def one(t, carry):
            wide = ref[t].astype(F32)
            power = jnp.mean(wide * wide, axis=-1, keepdims=True)
            y = (wide * lax.rsqrt(power + 1e-06) * gain_ref[...][None, :]).astype(BF)
            halves[0, at, t] = y[:, :HALF]
            halves[1, at, t] = y[:, HALF:]
            return carry

        lax.fori_loop(0, T, one, 0)

    def move_v(t, carry):
        halves[0, 2, t] = v_ref[t, :, :HALF]
        halves[1, 2, t] = v_ref[t, :, HALF:]
        return carry

    norm_into(q_ref, qg_ref, 0)
    norm_into(k_ref, kg_ref, 1)
    lax.fori_loop(0, T, move_v, 0)

    @pl.when(own)
    def _():
        pl.semaphore_wait(barrier, 2 * SLOTS)

    @pl.when(jnp.logical_not(own))
    def _():
        pl.semaphore_wait(barrier, 2 * SLOTS + 2)

    exch = []
    for at in range(3):
        cp = remote(halves.at[1 - c, at], mates.at[at], ex_s.at[at], ex_r.at[at], mate)
        cp.start()
        exch.append(cp)

    shape = (R, 2 * T, TILE)
    ow = lax.broadcasted_iota(jnp.int32, shape, 1)
    occ = (ow >= T).astype(jnp.int32)
    col = lax.broadcasted_iota(jnp.int32, (1, 1, TILE), 2)
    rank_of = jnp.zeros((1, 1, TILE), jnp.int32)
    for i in range(R):
        rank_of = jnp.where((col & 15) == i, ranks[i], rank_of)
    place_of = (col >> 4) + 64 * rank_of
    want = jnp.where(occ == c, 0, 1) * T + ow - T * occ
    want = want + 64 * lax.broadcasted_iota(jnp.int32, shape, 0)
    perm[...] = (want == place_of).astype(F32).reshape(TILE, TILE).astype(BF)

    lane0 = (lax.broadcasted_iota(jnp.int32, (SUB, HD), 1) == 0).astype(F32).astype(BF)

    def live_rows(slots, first, zpar):
        s = lax.broadcasted_iota(jnp.int32, (slots, 2 * T, HD), 0) + first
        flag = slot_pos((slots, 2 * T, HD), s, zpar) < count
        return flag.astype(F32).reshape(slots * 2 * T, HD)

    def masks(i, carry):
        flag = live_rows(16, (i & 3) * 16, jnp.where(i < 4, c, 1 - c))
        rows = pl.ds(pl.multiple_of(i * TILE, TILE), TILE)
        for h in range(3):
            ka[h, rows, HD:] = ((flag - 1.0) * 1e30).astype(BF)
            va[h, rows, HD:] = jnp.ones((TILE, HD), BF)
        return carry

    lax.fori_loop(0, 8, masks, 0)

    for at in range(3):
        exch[at].wait()

    def pack(at, xl, first, width):
        cols = slice(xl * 640 + first * HD, xl * 640 + (first + width) * HD)
        mine = halves[c, at, :, :, cols].reshape(T * R, width * HD)
        theirs = mates[at, :, :, cols].reshape(T * R, width * HD)
        both = jnp.concatenate([mine, theirs], axis=0)
        res = jnp.dot(perm[...], both, preferred_element_type=F32)
        return res.reshape(R, 2 * T, width * HD)

    parts = ((0, 4, 0), (4, 12, 1), (12, 16, 0))

    for at in range(3):
        for xl in range(2):
            for hp in range(2):
                res = pack(at, xl, 3 * hp, 2)
                two = jnp.concatenate([res[:, :, :HD], res[:, :, HD:]], axis=1).astype(BF)
                for lo, hi, odd in parts:
                    sb[lo:hi, xl, hp ^ odd ^ xl, at * 48 : at * 48 + 48, :] = two[lo:hi]

    far_ranks = R - cut
    if far_ranks:
        @pl.when(yl == 0)
        def _():
            remote(sb.at[pl.ds(cut, far_ranks), :, 1], rel, rel_s, rel_r, next_chip).start()

    def send_main(i, carry):
        k, xl, y2, to = dest(i)
        ok = jnp.logical_or(k < cut, jnp.logical_and(yl == 0, y2 == 0))

        @pl.when(ok)
        def _():
            send(sb.at[k, xl, y2], rb.at[slot], main_s, main_r.at[sgrp], to, is_self(i))

        return carry

    lax.fori_loop(0, SLOTS, send_main, 0)

    for xl in range(2):
        kv = jnp.concatenate([pack(1, xl, 2, 1), pack(2, xl, 2, 1)], axis=1)
        ss[:, xl, 0:48, :] = kv.astype(BF)
        qq = jnp.concatenate([pack(0, xl, 2, 1), jnp.zeros((R, 8, HD), F32)], axis=1)
        ss[:, xl, 48:80, :] = qq.astype(BF)

    def pass_on(k, xl, src, dst, ssem, rsem):
        gk = rank_group(k)
        here = jnp.logical_and(own, jnp.logical_and(g == gk, xl_me == xl))
        send(src, dst, ssem, rsem, (gk, 2 * c + xl, 2 + zp), here)

    def spare(k):
        return 1 ^ (rank_group(k) & 1)

    if far_ranks:
        @pl.when(yl == 0)
        def _():
            for k in range(cut, R):
                at = k - cut
                remote(
                    ss.at[k, spare(k)], rels.at[at], rels_s.at[at], rels_r.at[at], next_chip
                ).start()

        @pl.when(yl == 1)
        def _():
            wait_for(rel, rel_r)
            for k in range(cut, R):
                for xl in range(2):
                    pass_on(
                        k, xl, rel.at[k - cut, xl], rb.at[slot & 31], main_s, main_r.at[yh]
                    )

    def send_shared(i, carry):
        dr = i & 15
        xl = i >> 4
        ty = yh ^ (dr >> 3)
        tz = (z + dr) & 7
        k = group_rank(ty, tz)
        y2 = (tz & 1) ^ xl
        ok = jnp.logical_or(k < cut, jnp.logical_and(yl == 0, y2 == 0))
        here = jnp.logical_and(is_self(i), three)

        @pl.when(ok)
        def _():
            send(
                ss.at[k, xl], rsh.at[slot], sh_s, sh_r.at[sgrp],
                ((ty << 3) | tz, 2 * c + xl, y2 * 2 + zp), here,
            )

        return carry

    lax.fori_loop(0, SLOTS // 2, send_shared, 0)

    if far_ranks:
        @pl.when(yl == 1)
        def _():
            for k in range(cut, R):
                at = k - cut
                wait_for(rels.at[at], rels_r.at[at])
                pass_on(k, spare(k), rels.at[at], rsh.at[slot & 31], sh_s, sh_r.at[yh])

    def place(ref, h, rows, value):
        ref[h, rows, :HD] = value.reshape(TILE, HD).astype(BF)

    def gather(some, arrived, forward, ours, theirs, heads):
        def lay(i, value):
            rows = slice(i * TILE, (i + 1) * TILE)
            kv = value.astype(F32)
            for n, h in enumerate(heads):
                place(ka, h, rows, kv[:, 24 * n : 24 * n + 24])
                m = n + len(heads)
                place(va, h, rows, kv[:, 24 * m : 24 * m + 24])

        def blank(i):
            rows = slice(i * TILE, (i + 1) * TILE)
            for h in heads:
                ka[h, rows, :HD] = jnp.zeros((TILE, HD), BF)
                va[h, rows, :HD] = jnp.zeros((TILE, HD), BF)

        def first(i):
            arrived(i)
            forward(i).start()
            lay(i, ours(i))

        def second(i):
            forward(i).wait()
            lay(4 + i, theirs(i))

        for step, shift in ((first, 0), (second, 4)):
            for i in range(4):
                if i < 2 or not some:
                    step(i)
                else:
                    @pl.when(short)
                    def _(i=i, shift=shift):
                        blank(shift + i)

                    @pl.when(jnp.logical_not(short))
                    def _(i=i, step=step):
                        step(i)

    def grp(i):
        return pl.ds(16 * i, 16)

    gather(
        far_ranks,
        lambda i: wait_for(rb.at[grp(i)], main_r.at[i]),
        lambda i: remote(
            rb.at[grp(i), pl.ds(48, 96)], rm.at[grp(i)], fwd_s.at[i], fwd_r.at[i], mate
        ),
        lambda i: rb[16 * i : 16 * i + 16, 48:144, :],
        lambda i: rm[16 * i : 16 * i + 16],
        (0, 1),
    )

    scale = HD ** (-0.5) * LOG2E

    def attend(q, h, live):
        step = 512
        outs = []
        for n in range(BLOCK // SUB):
            rows = slice(n * SUB, (n + 1) * SUB)
            qa = jnp.concatenate([q[rows], lane0], axis=1)
            top = None
            for j in range(KEYS // step):
                cols = slice(j * step, (j + 1) * step)
                part = lax.dot_general(
                    qa, ka[h, cols, :], (((1,), (1,)), ((), ())),
                    preferred_element_type=F32,
                )
                scr[rows, cols] = part
                for i in range(step // HD):
                    piece = part[:, i * HD : (i + 1) * HD]
                    top = piece if top is None else jnp.maximum(top, piece)
            peak = jnp.max(top, axis=1, keepdims=True)
            mixed = None
            for j in range(KEYS // step):
                cols = slice(j * step, (j + 1) * step)
                weights = jnp.exp2((scr[rows, cols] - peak) * scale).astype(BF)
                part = jnp.dot(weights, va[h, cols, :], preferred_element_type=F32)
                mixed = part if mixed is None else mixed + part
            outs.append(jnp.where(live[rows] > 0.0, mixed[:, :HD] / mixed[:, HD:], 0.0))
        return jnp.concatenate(outs, axis=0)

    passes = jnp.where(short, 1, 2)

    def back_from(ref, to, ssem, rsem, first):
        def back(j, carry):
            s = first + j
            here = jnp.logical_and(own, s == slot)
            send(ref.at[s], to, ssem, rsem, source(s), here)
            return carry

        lax.fori_loop(0, 32, back, 0)

    def main_pass(i, carry):
        at = pl.ds(pl.multiple_of(i * 32, 32), 32)
        live = live_rows(32, i * 32, c)
        qq = rb[at, 0:48, :].astype(F32)
        res = []
        for h in range(2):
            q = qq[:, 24 * h : 24 * h + 24].reshape(BLOCK, HD).astype(BF)
            res.append(attend(q, h, live).reshape(32, 2 * T, HD))
        obs[at] = jnp.concatenate(res, axis=1).astype(BF)
        rsem = o_r.at[xl_me, short.astype(jnp.int32)]
        back_from(obs, ob.at[rank_me, xl_me, yl], o_s, rsem, i * 32)
        return carry

    lax.fori_loop(0, passes, main_pass, 0)

    def third_pass(i, carry):
        at = pl.ds(pl.multiple_of(i * 32, 32), 32)
        live = live_rows(32, i * 32, c)
        q = rsh[at, 48:80, :].astype(F32)[:, 0:24].reshape(BLOCK, HD).astype(BF)
        res = attend(q, 2, live).reshape(32, 2 * T, HD)
        oshs[at] = jnp.concatenate([res, jnp.zeros((32, 8, HD), F32)], axis=1).astype(BF)
        rsem = osh_r.at[xl_me, short.astype(jnp.int32)]
        back_from(oshs, osh.at[rank_me, xl_me], osh_s, rsem, i * 32)
        return carry

    def sent_back(ref, sem):
        whole = jnp.logical_not(short)
        one = jnp.logical_and(own, jnp.logical_or(whole, yl == 0))
        for n, kind in ((SLOTS, whole), (SLOTS // 2, short)):
            if n == SLOTS or far_ranks:
                @pl.when(jnp.logical_and(kind, one))
                def _(n=n):
                    wait_for(ref.at[pl.ds(0, n - 1)], sem)

                @pl.when(jnp.logical_and(kind, jnp.logical_not(one)))
                def _(n=n):
                    wait_for(ref.at[pl.ds(0, n)], sem)

    @pl.when(three)
    def _():
        gather(
            far_ranks,
            lambda i: wait_for(rsh.at[grp(i)], sh_r.at[i]),
            lambda i: remote(
                rsh.at[grp(i), pl.ds(0, 48)], rmsh.at[grp(i)], fsh_s.at[i], fsh_r.at[i], mate
            ),
            lambda i: rsh[16 * i : 16 * i + 16, 0:48, :],
            lambda i: rmsh[16 * i : 16 * i + 16],
            (2,),
        )
        lax.fori_loop(0, passes, third_pass, 0)
        sent_back(oshs, osh_s)

    sent_back(obs, o_s)
    n_main = SLOTS - 2 * far_ranks
    n_shared = SLOTS // 2 - far_ranks

    def sent(ref, n, sem, one):
        @pl.when(one)
        def _():
            wait_for(ref.at[pl.ds(0, n - 1)], sem)

        @pl.when(jnp.logical_not(one))
        def _():
            wait_for(ref.at[pl.ds(0, n)], sem)

    sent(rb, n_main, main_s, own)
    sent(rsh, n_shared, sh_s, jnp.logical_and(own, three))
    if far_ranks:
        @pl.when(yl == 0)
        def _():
            wait_for(rel, rel_s)
            for at in range(far_ranks):
                wait_for(rels.at[at], rels_s.at[at])

    def unpack(value):
        res = lax.dot_general(
            perm[...], value, (((0,), (0,)), ((), ())), preferred_element_type=F32
        )
        return res.astype(BF)

    def store(res, xl, first, width):
        cols = slice(xl * 640 + first * HD, xl * 640 + (first + width) * HD)
        fin[0, :, :, cols] = res[: T * R].reshape(T, R, width * HD)
        fin[1, :, :, cols] = res[T * R :].reshape(T, R, width * HD)

    def returned(ref, sem, xl):
        wait_for(ref.at[pl.ds(0, cut), xl], sem.at[xl, 0])
        if far_ranks:
            @pl.when(yl == 0)
            def _():
                wait_for(ref.at[pl.ds(cut, far_ranks), xl], sem.at[xl, 1])

            @pl.when(yl == 1)
            def _():
                ref[cut:, xl] = jnp.zeros(ref[cut:, xl].shape, BF)

    for xl in range(2):
        returned(ob, o_r, xl)
        for hp in range(2):
            got = jnp.concatenate(
                [ob[lo:hi, xl, hp ^ odd ^ xl] for lo, hi, odd in parts], axis=0
            ).astype(F32)
            flat = [got[:, 24 * h : 24 * h + 24].reshape(TILE, HD) for h in range(2)]
            store(unpack(jnp.concatenate(flat, axis=1).astype(BF)), xl, 3 * hp, 2)
    for xl in range(2):
        returned(osh, osh_r, xl)
        got = osh[:, xl].astype(F32)[:, 0:24].reshape(TILE, HD)
        store(unpack(got.astype(BF)), xl, 2, 1)

    cols = pl.ds(pl.multiple_of(c * HALF, HALF), HALF)
    far = remote(fin.at[1], out_ref.at[:, :, cols], fin_s, fin_r, mate)
    far.start()
    near = pltpu.make_async_copy(fin.at[0], out_ref.at[:, :, cols], fin_l)
    near.start()
    far.wait()
    near.wait()


def run(cut, lengths, q, k, v, q_gain, k_gain):
    vm = pl.BlockSpec(memory_space=pltpu.VMEM)
    dma = pltpu.SemaphoreType.DMA
    far = max(R - cut, 1)
    scratch = [
        pltpu.VMEM((2, 3, T, R, HALF), BF),
        pltpu.VMEM((3, T, R, HALF), BF),
        pltpu.VMEM((TILE, TILE), BF),
        pltpu.VMEM((R, 2, 2, 144, HD), BF),
        pltpu.VMEM((R, 2, 80, HD), BF),
        pltpu.VMEM((far, 2, 144, HD), BF),
        pltpu.VMEM((far, 80, HD), BF),
        pltpu.VMEM((SLOTS, 144, HD), BF),
        pltpu.VMEM((SLOTS, 80, HD), BF),
        pltpu.VMEM((SLOTS, 96, HD), BF),
        pltpu.VMEM((SLOTS, 48, HD), BF),
        pltpu.VMEM((3, KEYS, 2 * HD), BF),
        pltpu.VMEM((3, KEYS, 2 * HD), BF),
        pltpu.VMEM((BLOCK, KEYS), F32),
        pltpu.VMEM((SLOTS, 48, HD), BF),
        pltpu.VMEM((SLOTS, 32, HD), BF),
        pltpu.VMEM((R, 2, 2, 48, HD), BF),
        pltpu.VMEM((R, 2, 32, HD), BF),
        pltpu.VMEM((2, T, R, HALF), BF),
        dma((3,)), dma((3,)),
        dma, dma((4,)),
        dma((4,)), dma((4,)),
        dma, dma((4,)),
        dma((4,)), dma((4,)),
        dma, dma, dma((far,)), dma((far,)),
        dma, dma((2, 2)),
        dma, dma((2, 2)),
        dma, dma, dma,
    ]
    return pl.pallas_call(
        functools.partial(kernel, cut),
        out_shape=jax.ShapeDtypeStruct((T, R, 2 * HALF), BF),
        in_specs=[pl.BlockSpec(memory_space=pltpu.SMEM), vm, vm, vm, vm, vm],
        out_specs=pl.BlockSpec(memory_space=pl.ANY),
        scratch_shapes=scratch,
        compiler_params=pltpu.CompilerParams(
            collective_id=cut, has_side_effects=True, vmem_limit_bytes=60 << 20
        ),
        name="attend_%d" % cut,
    )(lengths, q, k, v, q_gain, k_gain)


def per_device(q_in, k_in, v_in, q_gain, k_gain, lengths):
    args = (
        lengths,
        jnp.transpose(q_in, (1, 0, 2)),
        jnp.transpose(k_in, (1, 0, 2)),
        jnp.transpose(v_in, (1, 0, 2)),
        q_gain,
        k_gain,
    )
    fits = jnp.sum((lengths > REACH).astype(jnp.int32)) <= CUT
    res = lax.cond(
        fits,
        functools.partial(run, CUT),
        functools.partial(run, R),
        *args,
    )
    return jnp.transpose(res, (1, 0, 2))


def solution(mesh):
    placed = P(None, ("grp", "uly", "blk"), None)
    return jax.shard_map(
        per_device,
        mesh=mesh,
        in_specs=(placed, placed, placed, P(), P(), P()),
        out_specs=placed,
        check_vma=False,
    )
```

```python
import functools
import math

import jax
import jax.numpy as jnp
from jax import lax
from jax.experimental import pallas as pl
from jax.experimental.pallas import tpu as pltpu
from jax.sharding import PartitionSpec as P

HD = 128
T = 12
R = 16
HALF = 1280
SLOTS = 64
KEYS = 3072
TILE = 384
BLOCK = 768
SUB = 256
REACH = 1536
CUTS = (10, 12, R)
LOG2E = math.log2(math.e)
MESH = pl.DeviceIdType.MESH
BF = jnp.bfloat16
F32 = jnp.float32


def slot_pos(shape, slot, zpar):
    w = lax.broadcasted_iota(jnp.int32, shape, 1)
    cc = (w >= T).astype(jnp.int32)
    t = w - T * cc
    x = slot & 3
    zh = (slot >> 2) & 3
    yh = (slot >> 4) & 1
    yl = slot >> 5
    z = zh * 2 + zpar
    return ((((yl * 2 + cc) * 4 + x) * 2 + yh) * 8 + z) * T + t


def group_rank(yh, z):
    k = (z >> 1) + (z & 1) * (4 + 2 * (1 - ((z >> 1) & 1)) - (z >> 1) + (z >> 2))
    return jnp.where((k & 1) == yh, k, 15 - k)


def rank_group(k):
    j = k if k < 8 else 15 - k
    z = 2 * j if j < 4 else (3, 7, 1, 5)[j - 4]
    yh = (j & 1) if k < 8 else 1 - (j & 1)
    return yh * 8 + z


def kernel(
    cut,
    len_ref, q_ref, k_ref, v_ref, qg_ref, kg_ref, out_ref,
    raw, halves, own_v, mates, perm, sb, ss, rel, rels, rb, rsh, rm, rmsh, ka, va, scr,
    obs, oshs, ob, osh, fin,
    ex_s, ex_r, main_s, main_r, fwd_s, fwd_r, sh_s, sh_r, fsh_s, fsh_r,
    rel_s, rel_r, rels_s, rels_r, o_s, o_r, osh_s, osh_r, fin_s, fin_r, fin_l, in_s,
):
    g = lax.axis_index("grp")
    x = lax.axis_index("uly")
    blk = lax.axis_index("blk")
    c = blk & 1
    yl = blk >> 1
    z = g & 7
    yh = g >> 3
    zp = z & 1
    zh = z >> 1
    slot = ((yl * 2 + yh) * 4 + zh) * 4 + x
    sgrp = slot >> 4
    xhalf = x >> 1
    xl_me = x & 1
    rank_me = group_rank(yh, z)
    short = rank_me >= cut
    three = yl == (zp ^ xl_me)
    mate = (g, x, yl * 2 + 1 - c)
    next_chip = (g, x, (1 - yl) * 2 + c)
    own = jnp.logical_and(xhalf == c, zp == c)

    def far_first(i):
        j = (i >> 2) & 7
        return (z + jnp.where((j & 1) == 0, 4 + (j >> 1), 3 - (j >> 1))) & 7

    def dest(i):
        xl = i & 1
        ty = yh ^ ((i >> 1) & 1)
        tz = far_first(i)
        y2 = yl ^ (i >> 5)
        return group_rank(ty, tz), xl, y2, ((ty << 3) | tz, 2 * c + xl, y2 * 2 + zp)

    def is_self(i):
        return jnp.logical_and(own, i == xl_me + 28)

    def source(s):
        return (
            (((s >> 4) & 1) << 3) | (((s >> 2) & 3) << 1) | c,
            s & 3,
            ((s >> 5) << 1) | xhalf,
        )

    def remote(src, dst, ssem, rsem, to):
        return pltpu.make_async_remote_copy(
            src_ref=src, dst_ref=dst, send_sem=ssem, recv_sem=rsem,
            device_id=to, device_id_type=MESH,
        )

    def send(src, dst, ssem, rsem, to, here):
        @pl.when(here)
        def _():
            pltpu.make_async_copy(src, dst, rsem).start()

        @pl.when(jnp.logical_not(here))
        def _():
            remote(src, dst, ssem, rsem, to).start()

    def wait_for(ref, sem):
        pltpu.make_async_copy(ref, ref, sem).wait()

    mine_cols = pl.ds(pl.multiple_of(c * HALF, HALF), HALF)
    mate_cols = pl.ds(pl.multiple_of((1 - c) * HALF, HALF), HALF)
    loads = [
        pltpu.make_async_copy(q_ref, raw.at[0], in_s.at[0]),
        pltpu.make_async_copy(k_ref, raw.at[1], in_s.at[1]),
        pltpu.make_async_copy(v_ref.at[:, :, mine_cols], own_v, in_s.at[2]),
    ]
    for load in loads:
        load.start()

    barrier = pltpu.get_barrier_semaphore()

    def greet(i, carry):
        @pl.when(jnp.logical_not(is_self(i)))
        def _():
            pl.semaphore_signal(barrier, inc=1, device_id=dest(i)[3], device_id_type=MESH)

        @pl.when(jnp.logical_not(jnp.logical_and(own, i == slot)))
        def _():
            pl.semaphore_signal(barrier, inc=1, device_id=source(i), device_id_type=MESH)

        return carry

    lax.fori_loop(0, SLOTS, greet, 0)
    pl.semaphore_signal(barrier, inc=1, device_id=mate, device_id_type=MESH)
    pl.semaphore_signal(barrier, inc=1, device_id=next_chip, device_id_type=MESH)

    sizes = [len_ref[i] for i in range(R)]
    ranks = []
    count = jnp.int32(0)
    for i in range(R):
        rank = jnp.int32(0)
        for j in range(R):
            if j != i:
                ahead = sizes[j] >= sizes[i] if j < i else sizes[j] > sizes[i]
                rank = rank + ahead.astype(jnp.int32)
        ranks.append(rank)
        count = count + jnp.where(rank == rank_me, sizes[i], 0)

    def norm_into(gain_ref, at):
        gain = gain_ref[...][None, :]
        for t in range(T):
            wide = raw[at, t].astype(F32)
            power = jnp.mean(wide * wide, axis=-1, keepdims=True)
            y = (wide * lax.rsqrt(power + 1e-06) * gain).astype(BF)
            halves[0, at, t] = y[:, :HALF]
            halves[1, at, t] = y[:, HALF:]

    loads[0].wait()
    norm_into(qg_ref, 0)

    @pl.when(own)
    def _():
        pl.semaphore_wait(barrier, 2 * SLOTS)

    @pl.when(jnp.logical_not(own))
    def _():
        pl.semaphore_wait(barrier, 2 * SLOTS + 2)

    exch = [
        remote(halves.at[1 - c, 0], mates.at[0], ex_s.at[0], ex_r.at[0], mate),
        remote(halves.at[1 - c, 1], mates.at[1], ex_s.at[1], ex_r.at[1], mate),
        remote(v_ref.at[:, :, mate_cols], mates.at[2], ex_s.at[2], ex_r.at[2], mate),
    ]
    exch[2].start()
    exch[0].start()
    loads[1].wait()
    norm_into(kg_ref, 1)
    exch[1].start()

    shape = (R, 2 * T, TILE)
    ow = lax.broadcasted_iota(jnp.int32, shape, 1)
    occ = (ow >= T).astype(jnp.int32)
    col = lax.broadcasted_iota(jnp.int32, (1, 1, TILE), 2)
    rank_of = jnp.zeros((1, 1, TILE), jnp.int32)
    for i in range(R):
        rank_of = jnp.where((col & 15) == i, ranks[i], rank_of)
    place_of = (col >> 4) + 64 * rank_of
    want = jnp.where(occ == c, 0, 1) * T + ow - T * occ
    want = want + 64 * lax.broadcasted_iota(jnp.int32, shape, 0)
    perm[...] = (want == place_of).astype(F32).reshape(TILE, TILE).astype(BF)

    loads[2].wait()
    for at in range(3):
        exch[at].wait()

    def pack(at, xl, first, width):
        cols = slice(xl * 640 + first * HD, xl * 640 + (first + width) * HD)
        mine = own_v[:, :, cols] if at == 2 else halves[c, at, :, :, cols]
        mine = mine.reshape(T * R, width * HD)
        theirs = mates[at, :, :, cols].reshape(T * R, width * HD)
        both = jnp.concatenate([mine, theirs], axis=0)
        res = jnp.dot(perm[...], both, preferred_element_type=F32)
        return res.reshape(R, 2 * T, width * HD)

    parts = ((0, 4, 0), (4, 12, 1), (12, 16, 0))

    for at in range(3):
        for xl in range(2):
            for hp in range(2):
                res = pack(at, xl, 3 * hp, 2)
                two = jnp.concatenate([res[:, :, :HD], res[:, :, HD:]], axis=1).astype(BF)
                for lo, hi, odd in parts:
                    sb[lo:hi, xl, hp ^ odd ^ xl, at * 48 : at * 48 + 48, :] = two[lo:hi]

    far_ranks = R - cut
    if far_ranks:
        @pl.when(yl == 0)
        def _():
            remote(sb.at[pl.ds(cut, far_ranks), :, 1], rel, rel_s, rel_r, next_chip).start()

    def send_main(i, carry):
        k, xl, y2, to = dest(i)
        ok = jnp.logical_or(k < cut, jnp.logical_and(yl == 0, y2 == 0))

        @pl.when(ok)
        def _():
            send(sb.at[k, xl, y2], rb.at[slot], main_s, main_r.at[sgrp], to, is_self(i))

        return carry

    lax.fori_loop(0, SLOTS, send_main, 0)

    for xl in range(2):
        kv = jnp.concatenate([pack(1, xl, 2, 1), pack(2, xl, 2, 1)], axis=1)
        ss[:, xl, 0:48, :] = kv.astype(BF)
        qq = jnp.concatenate([pack(0, xl, 2, 1), jnp.zeros((R, 8, HD), F32)], axis=1)
        ss[:, xl, 48:80, :] = qq.astype(BF)

    def pass_on(k, xl, src, dst, ssem, rsem):
        gk = rank_group(k)
        here = jnp.logical_and(own, jnp.logical_and(g == gk, xl_me == xl))
        send(src, dst, ssem, rsem, (gk, 2 * c + xl, 2 + zp), here)

    def spare(k):
        return 1 ^ (rank_group(k) & 1)

    if far_ranks:
        @pl.when(yl == 0)
        def _():
            for k in range(cut, R):
                at = k - cut
                remote(
                    ss.at[k, spare(k)], rels.at[at], rels_s.at[at], rels_r.at[at], next_chip
                ).start()

        @pl.when(yl == 1)
        def _():
            wait_for(rel, rel_r)
            for k in range(cut, R):
                for xl in range(2):
                    pass_on(
                        k, xl, rel.at[k - cut, xl], rb.at[slot & 31], main_s, main_r.at[yh]
                    )

    def send_shared(i, carry):
        xl = i & 1
        ty = yh ^ ((i >> 1) & 1)
        tz = far_first(i)
        k = group_rank(ty, tz)
        y2 = (tz & 1) ^ xl
        ok = jnp.logical_or(k < cut, jnp.logical_and(yl == 0, y2 == 0))
        here = jnp.logical_and(is_self(i), three)

        @pl.when(ok)
        def _():
            send(
                ss.at[k, xl], rsh.at[slot], sh_s, sh_r.at[sgrp],
                ((ty << 3) | tz, 2 * c + xl, y2 * 2 + zp), here,
            )

        return carry

    lax.fori_loop(0, SLOTS // 2, send_shared, 0)

    if far_ranks:
        @pl.when(yl == 1)
        def _():
            for k in range(cut, R):
                at = k - cut
                wait_for(rels.at[at], rels_r.at[at])
                pass_on(k, spare(k), rels.at[at], rsh.at[slot & 31], sh_s, sh_r.at[yh])

    lane0 = (lax.broadcasted_iota(jnp.int32, (SUB, HD), 1) == 0).astype(F32).astype(BF)

    def live_rows(slots, first, zpar):
        s = lax.broadcasted_iota(jnp.int32, (slots, 2 * T, HD), 0) + first
        flag = slot_pos((slots, 2 * T, HD), s, zpar) < count
        return flag.astype(F32).reshape(slots * 2 * T, HD)

    def masks(i, carry):
        flag = live_rows(16, (i & 3) * 16, jnp.where(i < 4, c, 1 - c))
        rows = pl.ds(pl.multiple_of(i * TILE, TILE), TILE)
        for h in range(3):
            ka[h, rows, HD:] = ((flag - 1.0) * 1e30).astype(BF)
            va[h, rows, HD:] = jnp.ones((TILE, HD), BF)
        return carry

    lax.fori_loop(0, 8, masks, 0)

    def place(ref, h, rows, value):
        ref[h, rows, :HD] = value.reshape(TILE, HD).astype(BF)

    def gather(some, arrived, forward, ours, theirs, heads):
        def lay(i, value):
            rows = slice(i * TILE, (i + 1) * TILE)
            kv = value.astype(F32)
            for n, h in enumerate(heads):
                place(ka, h, rows, kv[:, 24 * n : 24 * n + 24])
                m = n + len(heads)
                place(va, h, rows, kv[:, 24 * m : 24 * m + 24])

        def blank(i):
            rows = slice(i * TILE, (i + 1) * TILE)
            for h in heads:
                ka[h, rows, :HD] = jnp.zeros((TILE, HD), BF)
                va[h, rows, :HD] = jnp.zeros((TILE, HD), BF)

        def first(i):
            arrived(i)
            forward(i).start()
            lay(i, ours(i))

        def second(i):
            forward(i).wait()
            lay(4 + i, theirs(i))

        for step, shift in ((first, 0), (second, 4)):
            for i in range(4):
                if i < 2 or not some:
                    step(i)
                else:
                    @pl.when(short)
                    def _(i=i, shift=shift):
                        blank(shift + i)

                    @pl.when(jnp.logical_not(short))
                    def _(i=i, step=step):
                        step(i)

    def grp(i):
        return pl.ds(16 * i, 16)

    gather(
        far_ranks,
        lambda i: wait_for(rb.at[grp(i)], main_r.at[i]),
        lambda i: remote(
            rb.at[grp(i), pl.ds(48, 96)], rm.at[grp(i)], fwd_s.at[i], fwd_r.at[i], mate
        ),
        lambda i: rb[16 * i : 16 * i + 16, 48:144, :],
        lambda i: rm[16 * i : 16 * i + 16],
        (0, 1),
    )

    scale = HD ** (-0.5) * LOG2E

    def attend(q, h, live):
        step = 512
        outs = []
        for n in range(BLOCK // SUB):
            rows = slice(n * SUB, (n + 1) * SUB)
            qa = jnp.concatenate([q[rows], lane0], axis=1)
            top = None
            for j in range(KEYS // step):
                cols = slice(j * step, (j + 1) * step)
                part = lax.dot_general(
                    qa, ka[h, cols, :], (((1,), (1,)), ((), ())),
                    preferred_element_type=F32,
                )
                scr[rows, cols] = part
                for i in range(step // HD):
                    piece = part[:, i * HD : (i + 1) * HD]
                    top = piece if top is None else jnp.maximum(top, piece)
            peak = jnp.max(top, axis=1, keepdims=True)
            mixed = None
            for j in range(KEYS // step):
                cols = slice(j * step, (j + 1) * step)
                weights = jnp.exp2((scr[rows, cols] - peak) * scale).astype(BF)
                part = jnp.dot(weights, va[h, cols, :], preferred_element_type=F32)
                mixed = part if mixed is None else mixed + part
            outs.append(jnp.where(live[rows] > 0.0, mixed[:, :HD] / mixed[:, HD:], 0.0))
        return jnp.concatenate(outs, axis=0)

    passes = jnp.where(short, 1, 2)

    def back_from(ref, to, ssem, rsem, first):
        def back(j, carry):
            s = first + (j ^ (slot & 31))
            here = jnp.logical_and(own, s == slot)
            send(ref.at[s], to, ssem, rsem, source(s), here)
            return carry

        lax.fori_loop(0, 32, back, 0)

    def main_pass(i, carry):
        at = pl.ds(pl.multiple_of(i * 32, 32), 32)
        live = live_rows(32, i * 32, c)
        qq = rb[at, 0:48, :].astype(F32)
        res = []
        for h in range(2):
            q = qq[:, 24 * h : 24 * h + 24].reshape(BLOCK, HD).astype(BF)
            res.append(attend(q, h, live).reshape(32, 2 * T, HD))
        obs[at] = jnp.concatenate(res, axis=1).astype(BF)
        rsem = o_r.at[xl_me, short.astype(jnp.int32)]
        back_from(obs, ob.at[rank_me, xl_me, yl], o_s, rsem, i * 32)
        return carry

    lax.fori_loop(0, passes, main_pass, 0)

    def third_pass(i, carry):
        at = pl.ds(pl.multiple_of(i * 32, 32), 32)
        live = live_rows(32, i * 32, c)
        q = rsh[at, 48:80, :].astype(F32)[:, 0:24].reshape(BLOCK, HD).astype(BF)
        res = attend(q, 2, live).reshape(32, 2 * T, HD)
        oshs[at] = jnp.concatenate([res, jnp.zeros((32, 8, HD), F32)], axis=1).astype(BF)
        rsem = osh_r.at[xl_me, short.astype(jnp.int32)]
        back_from(oshs, osh.at[rank_me, xl_me], osh_s, rsem, i * 32)
        return carry

    def sent_back(ref, sem):
        whole = jnp.logical_not(short)
        one = jnp.logical_and(own, jnp.logical_or(whole, yl == 0))
        for n, kind in ((SLOTS, whole), (SLOTS // 2, short)):
            if n == SLOTS or far_ranks:
                @pl.when(jnp.logical_and(kind, one))
                def _(n=n):
                    wait_for(ref.at[pl.ds(0, n - 1)], sem)

                @pl.when(jnp.logical_and(kind, jnp.logical_not(one)))
                def _(n=n):
                    wait_for(ref.at[pl.ds(0, n)], sem)

    @pl.when(three)
    def _():
        gather(
            far_ranks,
            lambda i: wait_for(rsh.at[grp(i)], sh_r.at[i]),
            lambda i: remote(
                rsh.at[grp(i), pl.ds(0, 48)], rmsh.at[grp(i)], fsh_s.at[i], fsh_r.at[i], mate
            ),
            lambda i: rsh[16 * i : 16 * i + 16, 0:48, :],
            lambda i: rmsh[16 * i : 16 * i + 16],
            (2,),
        )
        lax.fori_loop(0, passes, third_pass, 0)
        sent_back(oshs, osh_s)

    sent_back(obs, o_s)
    n_main = SLOTS - 2 * far_ranks
    n_shared = SLOTS // 2 - far_ranks

    def sent(ref, n, sem, one):
        @pl.when(one)
        def _():
            wait_for(ref.at[pl.ds(0, n - 1)], sem)

        @pl.when(jnp.logical_not(one))
        def _():
            wait_for(ref.at[pl.ds(0, n)], sem)

    sent(rb, n_main, main_s, own)
    sent(rsh, n_shared, sh_s, jnp.logical_and(own, three))
    if far_ranks:
        @pl.when(yl == 0)
        def _():
            wait_for(rel, rel_s)
            for at in range(far_ranks):
                wait_for(rels.at[at], rels_s.at[at])

    def unpack(value):
        res = lax.dot_general(
            perm[...], value, (((0,), (0,)), ((), ())), preferred_element_type=F32
        )
        return res.astype(BF)

    def store(res, xl, first, width):
        cols = slice(xl * 640 + first * HD, xl * 640 + (first + width) * HD)
        fin[0, :, :, cols] = res[: T * R].reshape(T, R, width * HD)
        fin[1, :, :, cols] = res[T * R :].reshape(T, R, width * HD)

    def returned(ref, sem, xl):
        wait_for(ref.at[pl.ds(0, cut), xl], sem.at[xl, 0])
        if far_ranks:
            @pl.when(yl == 0)
            def _():
                wait_for(ref.at[pl.ds(cut, far_ranks), xl], sem.at[xl, 1])

            @pl.when(yl == 1)
            def _():
                ref[cut:, xl] = jnp.zeros(ref[cut:, xl].shape, BF)

    done = []

    def ship(first, width):
        n = len(done)
        at = pl.ds(pl.multiple_of(c * HALF + first, HD), width)
        here = pl.ds(first, width)
        far = remote(
            fin.at[1, :, :, here], out_ref.at[:, :, at], fin_s.at[n], fin_r.at[n], mate
        )
        far.start()
        near = pltpu.make_async_copy(fin.at[0, :, :, here], out_ref.at[:, :, at], fin_l.at[n])
        near.start()
        done.append((far, near))

    for xl in range(2):
        returned(ob, o_r, xl)
        for hp in range(2):
            got = jnp.concatenate(
                [ob[lo:hi, xl, hp ^ odd ^ xl] for lo, hi, odd in parts], axis=0
            ).astype(F32)
            flat = [got[:, 24 * h : 24 * h + 24].reshape(TILE, HD) for h in range(2)]
            store(unpack(jnp.concatenate(flat, axis=1).astype(BF)), xl, 3 * hp, 2)
            ship(xl * 640 + 384 * hp, 256)
    for xl in range(2):
        returned(osh, osh_r, xl)
        got = osh[:, xl].astype(F32)[:, 0:24].reshape(TILE, HD)
        store(unpack(got.astype(BF)), xl, 2, 1)
        ship(xl * 640 + 256, 128)
    for far, near in done:
        far.wait()
        near.wait()


def run(cut, lengths, q, k, v, q_gain, k_gain):
    vm = pl.BlockSpec(memory_space=pltpu.VMEM)
    hbm = pl.BlockSpec(memory_space=pl.ANY)
    dma = pltpu.SemaphoreType.DMA
    far = max(R - cut, 1)
    scratch = [
        pltpu.VMEM((2, T, R, 2 * HALF), BF),
        pltpu.VMEM((2, 2, T, R, HALF), BF),
        pltpu.VMEM((T, R, HALF), BF),
        pltpu.VMEM((3, T, R, HALF), BF),
        pltpu.VMEM((TILE, TILE), BF),
        pltpu.VMEM((R, 2, 2, 144, HD), BF),
        pltpu.VMEM((R, 2, 80, HD), BF),
        pltpu.VMEM((far, 2, 144, HD), BF),
        pltpu.VMEM((far, 80, HD), BF),
        pltpu.VMEM((SLOTS, 144, HD), BF),
        pltpu.VMEM((SLOTS, 80, HD), BF),
        pltpu.VMEM((SLOTS, 96, HD), BF),
        pltpu.VMEM((SLOTS, 48, HD), BF),
        pltpu.VMEM((3, KEYS, 2 * HD), BF),
        pltpu.VMEM((3, KEYS, 2 * HD), BF),
        pltpu.VMEM((BLOCK, KEYS), F32),
        pltpu.VMEM((SLOTS, 48, HD), BF),
        pltpu.VMEM((SLOTS, 32, HD), BF),
        pltpu.VMEM((R, 2, 2, 48, HD), BF),
        pltpu.VMEM((R, 2, 32, HD), BF),
        pltpu.VMEM((2, T, R, HALF), BF),
        dma((3,)), dma((3,)),
        dma, dma((4,)),
        dma((4,)), dma((4,)),
        dma, dma((4,)),
        dma((4,)), dma((4,)),
        dma, dma, dma((far,)), dma((far,)),
        dma, dma((2, 2)),
        dma, dma((2, 2)),
        dma((6,)), dma((6,)), dma((6,)),
        dma((3,)),
    ]
    return pl.pallas_call(
        functools.partial(kernel, cut),
        out_shape=jax.ShapeDtypeStruct((T, R, 2 * HALF), BF),
        in_specs=[pl.BlockSpec(memory_space=pltpu.SMEM), hbm, hbm, hbm, vm, vm],
        out_specs=pl.BlockSpec(memory_space=pl.ANY),
        scratch_shapes=scratch,
        compiler_params=pltpu.CompilerParams(
            collective_id=cut, has_side_effects=True, vmem_limit_bytes=60 << 20
        ),
        name="attend_%d" % cut,
    )(lengths, q, k, v, q_gain, k_gain)


def per_device(q_in, k_in, v_in, q_gain, k_gain, lengths):
    args = (
        lengths,
        jnp.transpose(q_in, (1, 0, 2)),
        jnp.transpose(k_in, (1, 0, 2)),
        jnp.transpose(v_in, (1, 0, 2)),
        q_gain,
        k_gain,
    )
    long = jnp.sum((lengths > REACH).astype(jnp.int32))
    which = sum((long > cut).astype(jnp.int32) for cut in CUTS[:-1])
    res = lax.switch(which, [functools.partial(run, cut) for cut in CUTS], *args)
    return jnp.transpose(res, (1, 0, 2))


def solution(mesh):
    placed = P(None, ("grp", "uly", "blk"), None)
    return jax.shard_map(
        per_device,
        mesh=mesh,
        in_specs=(placed, placed, placed, P(), P(), P()),
        out_specs=placed,
        check_vma=False,
    )
```

```python
import functools
import math

import jax
import jax.numpy as jnp
from jax import lax
from jax.experimental import pallas as pl
from jax.experimental.pallas import tpu as pltpu
from jax.sharding import PartitionSpec as P

HD = 128
T = 12
R = 16
HALF = 1280
SLOTS = 64
KEYS = 3072
TILE = 384
BLOCK = 768
SUB = 256
REACH = 1536
CUT = 10
LOG2E = math.log2(math.e)
MESH = pl.DeviceIdType.MESH
BF = jnp.bfloat16
F32 = jnp.float32


def slot_pos(shape, slot, zpar):
    w = lax.broadcasted_iota(jnp.int32, shape, 1)
    cc = (w >= T).astype(jnp.int32)
    t = w - T * cc
    x = slot & 3
    zh = (slot >> 2) & 3
    yh = (slot >> 4) & 1
    yl = slot >> 5
    z = zh * 2 + zpar
    return ((((yl * 2 + cc) * 4 + x) * 2 + yh) * 8 + z) * T + t


def group_rank(yh, z):
    k = (z >> 1) + (z & 1) * (4 + 2 * (1 - ((z >> 1) & 1)) - (z >> 1) + (z >> 2))
    return jnp.where((k & 1) == yh, k, 15 - k)


def rank_group(k):
    j = k if k < 8 else 15 - k
    z = 2 * j if j < 4 else (3, 7, 1, 5)[j - 4]
    yh = (j & 1) if k < 8 else 1 - (j & 1)
    return yh * 8 + z


def kernel(
    cut,
    len_ref, q_ref, k_ref, v_ref, qg_ref, kg_ref, out_ref,
    raw, halves, own_v, mates, perm, sb, ss, rel, rels, rb, rsh, rm, rmsh, ka, va, scr,
    obs, oshs, ob, osh, fin,
    ex_s, ex_r, main_s, main_r, fwd_s, fwd_r, sh_s, sh_r, fsh_s, fsh_r,
    rel_s, rel_r, rels_s, rels_r, o_s, o_r, osh_s, osh_r, fin_s, fin_r, fin_l, in_s,
):
    g = lax.axis_index("grp")
    x = lax.axis_index("uly")
    blk = lax.axis_index("blk")
    c = blk & 1
    yl = blk >> 1
    z = g & 7
    yh = g >> 3
    zp = z & 1
    zh = z >> 1
    slot = ((yl * 2 + yh) * 4 + zh) * 4 + x
    sgrp = slot >> 4
    xhalf = x >> 1
    xl_me = x & 1
    rank_me = group_rank(yh, z)
    short = rank_me >= cut
    three = yl == (zp ^ xl_me)
    mate = (g, x, yl * 2 + 1 - c)
    next_chip = (g, x, (1 - yl) * 2 + c)
    own = jnp.logical_and(xhalf == c, zp == c)

    def far_first(i):
        j = (i >> 2) & 7
        return (z + jnp.where((j & 1) == 0, 4 + (j >> 1), 3 - (j >> 1))) & 7

    def dest(i):
        xl = i & 1
        ty = yh ^ ((i >> 1) & 1)
        tz = far_first(i)
        y2 = yl ^ (i >> 5)
        return group_rank(ty, tz), xl, y2, ((ty << 3) | tz, 2 * c + xl, y2 * 2 + zp)

    def is_self(i):
        return jnp.logical_and(own, i == xl_me + 28)

    def source(s):
        return (
            (((s >> 4) & 1) << 3) | (((s >> 2) & 3) << 1) | c,
            s & 3,
            ((s >> 5) << 1) | xhalf,
        )

    def remote(src, dst, ssem, rsem, to):
        return pltpu.make_async_remote_copy(
            src_ref=src, dst_ref=dst, send_sem=ssem, recv_sem=rsem,
            device_id=to, device_id_type=MESH,
        )

    def send(src, dst, ssem, rsem, to, here):
        @pl.when(here)
        def _():
            pltpu.make_async_copy(src, dst, rsem).start()

        @pl.when(jnp.logical_not(here))
        def _():
            remote(src, dst, ssem, rsem, to).start()

    def wait_for(ref, sem):
        pltpu.make_async_copy(ref, ref, sem).wait()

    mine_cols = pl.ds(pl.multiple_of(c * HALF, HALF), HALF)
    mate_cols = pl.ds(pl.multiple_of((1 - c) * HALF, HALF), HALF)
    loads = [
        pltpu.make_async_copy(q_ref, raw.at[0], in_s.at[0]),
        pltpu.make_async_copy(k_ref, raw.at[1], in_s.at[1]),
        pltpu.make_async_copy(v_ref.at[:, :, mine_cols], own_v, in_s.at[2]),
    ]
    for load in loads:
        load.start()

    barrier = pltpu.get_barrier_semaphore()

    def greet(i, carry):
        @pl.when(jnp.logical_not(is_self(i)))
        def _():
            pl.semaphore_signal(barrier, inc=1, device_id=dest(i)[3], device_id_type=MESH)

        @pl.when(jnp.logical_not(jnp.logical_and(own, i == slot)))
        def _():
            pl.semaphore_signal(barrier, inc=1, device_id=source(i), device_id_type=MESH)

        return carry

    lax.fori_loop(0, SLOTS, greet, 0)
    pl.semaphore_signal(barrier, inc=1, device_id=mate, device_id_type=MESH)
    pl.semaphore_signal(barrier, inc=1, device_id=next_chip, device_id_type=MESH)

    sizes = [len_ref[i] for i in range(R)]
    ranks = []
    count = jnp.int32(0)
    for i in range(R):
        rank = jnp.int32(0)
        for j in range(R):
            if j != i:
                ahead = sizes[j] >= sizes[i] if j < i else sizes[j] > sizes[i]
                rank = rank + ahead.astype(jnp.int32)
        ranks.append(rank)
        count = count + jnp.where(rank == rank_me, sizes[i], 0)

    def norm_into(gain_ref, at):
        gain = gain_ref[...][None, :]
        for t in range(T):
            wide = raw[at, t].astype(F32)
            power = jnp.mean(wide * wide, axis=-1, keepdims=True)
            y = (wide * lax.rsqrt(power + 1e-06) * gain).astype(BF)
            halves[0, at, t] = y[:, :HALF]
            halves[1, at, t] = y[:, HALF:]

    loads[0].wait()
    norm_into(qg_ref, 0)

    @pl.when(own)
    def _():
        pl.semaphore_wait(barrier, 2 * SLOTS)

    @pl.when(jnp.logical_not(own))
    def _():
        pl.semaphore_wait(barrier, 2 * SLOTS + 2)

    exch = [
        remote(halves.at[1 - c, 0], mates.at[0], ex_s.at[0], ex_r.at[0], mate),
        remote(halves.at[1 - c, 1], mates.at[1], ex_s.at[1], ex_r.at[1], mate),
        remote(v_ref.at[:, :, mate_cols], mates.at[2], ex_s.at[2], ex_r.at[2], mate),
    ]
    exch[2].start()
    exch[0].start()
    loads[1].wait()
    norm_into(kg_ref, 1)
    exch[1].start()

    shape = (R, 2 * T, TILE)
    ow = lax.broadcasted_iota(jnp.int32, shape, 1)
    occ = (ow >= T).astype(jnp.int32)
    col = lax.broadcasted_iota(jnp.int32, (1, 1, TILE), 2)
    rank_of = jnp.zeros((1, 1, TILE), jnp.int32)
    for i in range(R):
        rank_of = jnp.where((col & 15) == i, ranks[i], rank_of)
    place_of = (col >> 4) + 64 * rank_of
    want = jnp.where(occ == c, 0, 1) * T + ow - T * occ
    want = want + 64 * lax.broadcasted_iota(jnp.int32, shape, 0)
    perm[...] = (want == place_of).astype(F32).reshape(TILE, TILE).astype(BF)

    loads[2].wait()
    for at in range(3):
        exch[at].wait()

    def pack(at, xl, first, width):
        cols = slice(xl * 640 + first * HD, xl * 640 + (first + width) * HD)
        mine = own_v[:, :, cols] if at == 2 else halves[c, at, :, :, cols]
        mine = mine.reshape(T * R, width * HD)
        theirs = mates[at, :, :, cols].reshape(T * R, width * HD)
        both = jnp.concatenate([mine, theirs], axis=0)
        res = jnp.dot(perm[...], both, preferred_element_type=F32)
        return res.reshape(R, 2 * T, width * HD)

    parts = ((0, 4, 0), (4, 12, 1), (12, 16, 0))

    for at in range(3):
        for xl in range(2):
            for hp in range(2):
                res = pack(at, xl, 3 * hp, 2)
                two = jnp.concatenate([res[:, :, :HD], res[:, :, HD:]], axis=1).astype(BF)
                for lo, hi, odd in parts:
                    sb[lo:hi, xl, hp ^ odd ^ xl, at * 48 : at * 48 + 48, :] = two[lo:hi]

    far_ranks = R - cut
    if far_ranks:
        @pl.when(yl == 0)
        def _():
            remote(sb.at[pl.ds(cut, far_ranks), :, 1], rel, rel_s, rel_r, next_chip).start()

    def send_main(i, carry):
        k, xl, y2, to = dest(i)
        ok = jnp.logical_or(k < cut, jnp.logical_and(yl == 0, y2 == 0))

        @pl.when(ok)
        def _():
            send(sb.at[k, xl, y2], rb.at[slot], main_s, main_r.at[sgrp], to, is_self(i))

        return carry

    lax.fori_loop(0, SLOTS, send_main, 0)

    for xl in range(2):
        kv = jnp.concatenate([pack(1, xl, 2, 1), pack(2, xl, 2, 1)], axis=1)
        ss[:, xl, 0:48, :] = kv.astype(BF)
        qq = jnp.concatenate([pack(0, xl, 2, 1), jnp.zeros((R, 8, HD), F32)], axis=1)
        ss[:, xl, 48:80, :] = qq.astype(BF)

    def pass_on(k, xl, src, dst, ssem, rsem):
        gk = rank_group(k)
        here = jnp.logical_and(own, jnp.logical_and(g == gk, xl_me == xl))
        send(src, dst, ssem, rsem, (gk, 2 * c + xl, 2 + zp), here)

    def spare(k):
        return 1 ^ (rank_group(k) & 1)

    if far_ranks:
        @pl.when(yl == 0)
        def _():
            for k in range(cut, R):
                at = k - cut
                remote(
                    ss.at[k, spare(k)], rels.at[at], rels_s.at[at], rels_r.at[at], next_chip
                ).start()

        @pl.when(yl == 1)
        def _():
            wait_for(rel, rel_r)
            for k in range(cut, R):
                for xl in range(2):
                    pass_on(
                        k, xl, rel.at[k - cut, xl], rb.at[slot & 31], main_s, main_r.at[yh]
                    )

    def send_shared(i, carry):
        xl = i & 1
        ty = yh ^ ((i >> 1) & 1)
        tz = far_first(i)
        k = group_rank(ty, tz)
        y2 = (tz & 1) ^ xl
        ok = jnp.logical_or(k < cut, jnp.logical_and(yl == 0, y2 == 0))
        here = jnp.logical_and(is_self(i), three)

        @pl.when(ok)
        def _():
            send(
                ss.at[k, xl], rsh.at[slot], sh_s, sh_r.at[sgrp],
                ((ty << 3) | tz, 2 * c + xl, y2 * 2 + zp), here,
            )

        return carry

    lax.fori_loop(0, SLOTS // 2, send_shared, 0)

    if far_ranks:
        @pl.when(yl == 1)
        def _():
            for k in range(cut, R):
                at = k - cut
                wait_for(rels.at[at], rels_r.at[at])
                pass_on(k, spare(k), rels.at[at], rsh.at[slot & 31], sh_s, sh_r.at[yh])

    lane0 = (lax.broadcasted_iota(jnp.int32, (SUB, HD), 1) == 0).astype(F32).astype(BF)

    def live_rows(slots, first, zpar):
        s = lax.broadcasted_iota(jnp.int32, (slots, 2 * T, HD), 0) + first
        flag = slot_pos((slots, 2 * T, HD), s, zpar) < count
        return flag.astype(F32).reshape(slots * 2 * T, HD)

    def masks(i, carry):
        flag = live_rows(16, (i & 3) * 16, jnp.where(i < 4, c, 1 - c))
        rows = pl.ds(pl.multiple_of(i * TILE, TILE), TILE)
        for h in range(3):
            ka[h, rows, HD:] = ((flag - 1.0) * 1e30).astype(BF)
            va[h, rows, HD:] = jnp.ones((TILE, HD), BF)
        return carry

    lax.fori_loop(0, 8, masks, 0)

    def place(ref, h, rows, value):
        ref[h, rows, :HD] = value.reshape(TILE, HD).astype(BF)

    def gather(some, arrived, forward, ours, theirs, heads):
        def lay(i, value):
            rows = slice(i * TILE, (i + 1) * TILE)
            kv = value.astype(F32)
            for n, h in enumerate(heads):
                place(ka, h, rows, kv[:, 24 * n : 24 * n + 24])
                m = n + len(heads)
                place(va, h, rows, kv[:, 24 * m : 24 * m + 24])

        def blank(i):
            rows = slice(i * TILE, (i + 1) * TILE)
            for h in heads:
                ka[h, rows, :HD] = jnp.zeros((TILE, HD), BF)
                va[h, rows, :HD] = jnp.zeros((TILE, HD), BF)

        def first(i):
            arrived(i)
            forward(i).start()
            lay(i, ours(i))

        def second(i):
            forward(i).wait()
            lay(4 + i, theirs(i))

        for step, shift in ((first, 0), (second, 4)):
            for i in range(4):
                if i < 2 or not some:
                    step(i)
                else:
                    @pl.when(short)
                    def _(i=i, shift=shift):
                        blank(shift + i)

                    @pl.when(jnp.logical_not(short))
                    def _(i=i, step=step):
                        step(i)

    def grp(i):
        return pl.ds(16 * i, 16)

    gather(
        far_ranks,
        lambda i: wait_for(rb.at[grp(i)], main_r.at[i]),
        lambda i: remote(
            rb.at[grp(i), pl.ds(48, 96)], rm.at[grp(i)], fwd_s.at[i], fwd_r.at[i], mate
        ),
        lambda i: rb[16 * i : 16 * i + 16, 48:144, :],
        lambda i: rm[16 * i : 16 * i + 16],
        (0, 1),
    )

    scale = HD ** (-0.5) * LOG2E

    def attend(q, h, live):
        step = 512
        outs = []
        for n in range(BLOCK // SUB):
            rows = slice(n * SUB, (n + 1) * SUB)
            qa = jnp.concatenate([q[rows], lane0], axis=1)
            top = None
            for j in range(KEYS // step):
                cols = slice(j * step, (j + 1) * step)
                part = lax.dot_general(
                    qa, ka[h, cols, :], (((1,), (1,)), ((), ())),
                    preferred_element_type=F32,
                )
                scr[rows, cols] = part
                for i in range(step // HD):
                    piece = part[:, i * HD : (i + 1) * HD]
                    top = piece if top is None else jnp.maximum(top, piece)
            peak = jnp.max(top, axis=1, keepdims=True)
            mixed = None
            for j in range(KEYS // step):
                cols = slice(j * step, (j + 1) * step)
                weights = jnp.exp2((scr[rows, cols] - peak) * scale).astype(BF)
                part = jnp.dot(weights, va[h, cols, :], preferred_element_type=F32)
                mixed = part if mixed is None else mixed + part
            outs.append(jnp.where(live[rows] > 0.0, mixed[:, :HD] / mixed[:, HD:], 0.0))
        return jnp.concatenate(outs, axis=0)

    passes = jnp.where(short, 1, 2)

    def back_from(ref, to, ssem, rsem, first):
        def back(j, carry):
            s = first + (j ^ (slot & 31))
            here = jnp.logical_and(own, s == slot)
            send(ref.at[s], to, ssem, rsem, source(s), here)
            return carry

        lax.fori_loop(0, 32, back, 0)

    def main_pass(i, carry):
        at = pl.ds(pl.multiple_of(i * 32, 32), 32)
        live = live_rows(32, i * 32, c)
        qq = rb[at, 0:48, :].astype(F32)
        res = []
        for h in range(2):
            q = qq[:, 24 * h : 24 * h + 24].reshape(BLOCK, HD).astype(BF)
            res.append(attend(q, h, live).reshape(32, 2 * T, HD))
        obs[at] = jnp.concatenate(res, axis=1).astype(BF)
        rsem = o_r.at[xl_me, short.astype(jnp.int32)]
        back_from(obs, ob.at[rank_me, xl_me, yl], o_s, rsem, i * 32)
        return carry

    lax.fori_loop(0, passes, main_pass, 0)

    def third_pass(i, carry):
        at = pl.ds(pl.multiple_of(i * 32, 32), 32)
        live = live_rows(32, i * 32, c)
        q = rsh[at, 48:80, :].astype(F32)[:, 0:24].reshape(BLOCK, HD).astype(BF)
        res = attend(q, 2, live).reshape(32, 2 * T, HD)
        oshs[at] = jnp.concatenate([res, jnp.zeros((32, 8, HD), F32)], axis=1).astype(BF)
        rsem = osh_r.at[xl_me, short.astype(jnp.int32)]
        back_from(oshs, osh.at[rank_me, xl_me], osh_s, rsem, i * 32)
        return carry

    def sent_back(ref, sem):
        whole = jnp.logical_not(short)
        one = jnp.logical_and(own, jnp.logical_or(whole, yl == 0))
        for n, kind in ((SLOTS, whole), (SLOTS // 2, short)):
            if n == SLOTS or far_ranks:
                @pl.when(jnp.logical_and(kind, one))
                def _(n=n):
                    wait_for(ref.at[pl.ds(0, n - 1)], sem)

                @pl.when(jnp.logical_and(kind, jnp.logical_not(one)))
                def _(n=n):
                    wait_for(ref.at[pl.ds(0, n)], sem)

    @pl.when(three)
    def _():
        gather(
            far_ranks,
            lambda i: wait_for(rsh.at[grp(i)], sh_r.at[i]),
            lambda i: remote(
                rsh.at[grp(i), pl.ds(0, 48)], rmsh.at[grp(i)], fsh_s.at[i], fsh_r.at[i], mate
            ),
            lambda i: rsh[16 * i : 16 * i + 16, 0:48, :],
            lambda i: rmsh[16 * i : 16 * i + 16],
            (2,),
        )
        lax.fori_loop(0, passes, third_pass, 0)
        sent_back(oshs, osh_s)

    sent_back(obs, o_s)
    n_main = SLOTS - 2 * far_ranks
    n_shared = SLOTS // 2 - far_ranks

    def sent(ref, n, sem, one):
        @pl.when(one)
        def _():
            wait_for(ref.at[pl.ds(0, n - 1)], sem)

        @pl.when(jnp.logical_not(one))
        def _():
            wait_for(ref.at[pl.ds(0, n)], sem)

    sent(rb, n_main, main_s, own)
    sent(rsh, n_shared, sh_s, jnp.logical_and(own, three))
    if far_ranks:
        @pl.when(yl == 0)
        def _():
            wait_for(rel, rel_s)
            for at in range(far_ranks):
                wait_for(rels.at[at], rels_s.at[at])

    def unpack(value):
        res = lax.dot_general(
            perm[...], value, (((0,), (0,)), ((), ())), preferred_element_type=F32
        )
        return res.astype(BF)

    def store(res, xl, first, width):
        cols = slice(xl * 640 + first * HD, xl * 640 + (first + width) * HD)
        fin[0, :, :, cols] = res[: T * R].reshape(T, R, width * HD)
        fin[1, :, :, cols] = res[T * R :].reshape(T, R, width * HD)

    def returned(ref, sem, xl):
        wait_for(ref.at[pl.ds(0, cut), xl], sem.at[xl, 0])
        if far_ranks:
            @pl.when(yl == 0)
            def _():
                wait_for(ref.at[pl.ds(cut, far_ranks), xl], sem.at[xl, 1])

            @pl.when(yl == 1)
            def _():
                ref[cut:, xl] = jnp.zeros(ref[cut:, xl].shape, BF)

    done = []

    def ship(first, width):
        n = len(done)
        at = pl.ds(pl.multiple_of(c * HALF + first, HD), width)
        here = pl.ds(first, width)
        far = remote(
            fin.at[1, :, :, here], out_ref.at[:, :, at], fin_s.at[n], fin_r.at[n], mate
        )
        far.start()
        near = pltpu.make_async_copy(fin.at[0, :, :, here], out_ref.at[:, :, at], fin_l.at[n])
        near.start()
        done.append((far, near))

    for xl in range(2):
        returned(ob, o_r, xl)
        for hp in range(2):
            got = jnp.concatenate(
                [ob[lo:hi, xl, hp ^ odd ^ xl] for lo, hi, odd in parts], axis=0
            ).astype(F32)
            flat = [got[:, 24 * h : 24 * h + 24].reshape(TILE, HD) for h in range(2)]
            store(unpack(jnp.concatenate(flat, axis=1).astype(BF)), xl, 3 * hp, 2)
            ship(xl * 640 + 384 * hp, 256)
    for xl in range(2):
        returned(osh, osh_r, xl)
        got = osh[:, xl].astype(F32)[:, 0:24].reshape(TILE, HD)
        store(unpack(got.astype(BF)), xl, 2, 1)
        ship(xl * 640 + 256, 128)
    for far, near in done:
        far.wait()
        near.wait()


def run(cut, lengths, q, k, v, q_gain, k_gain):
    vm = pl.BlockSpec(memory_space=pltpu.VMEM)
    hbm = pl.BlockSpec(memory_space=pl.ANY)
    dma = pltpu.SemaphoreType.DMA
    far = max(R - cut, 1)
    scratch = [
        pltpu.VMEM((2, T, R, 2 * HALF), BF),
        pltpu.VMEM((2, 2, T, R, HALF), BF),
        pltpu.VMEM((T, R, HALF), BF),
        pltpu.VMEM((3, T, R, HALF), BF),
        pltpu.VMEM((TILE, TILE), BF),
        pltpu.VMEM((R, 2, 2, 144, HD), BF),
        pltpu.VMEM((R, 2, 80, HD), BF),
        pltpu.VMEM((far, 2, 144, HD), BF),
        pltpu.VMEM((far, 80, HD), BF),
        pltpu.VMEM((SLOTS, 144, HD), BF),
        pltpu.VMEM((SLOTS, 80, HD), BF),
        pltpu.VMEM((SLOTS, 96, HD), BF),
        pltpu.VMEM((SLOTS, 48, HD), BF),
        pltpu.VMEM((3, KEYS, 2 * HD), BF),
        pltpu.VMEM((3, KEYS, 2 * HD), BF),
        pltpu.VMEM((BLOCK, KEYS), F32),
        pltpu.VMEM((SLOTS, 48, HD), BF),
        pltpu.VMEM((SLOTS, 32, HD), BF),
        pltpu.VMEM((R, 2, 2, 48, HD), BF),
        pltpu.VMEM((R, 2, 32, HD), BF),
        pltpu.VMEM((2, T, R, HALF), BF),
        dma((3,)), dma((3,)),
        dma, dma((4,)),
        dma((4,)), dma((4,)),
        dma, dma((4,)),
        dma((4,)), dma((4,)),
        dma, dma, dma((far,)), dma((far,)),
        dma, dma((2, 2)),
        dma, dma((2, 2)),
        dma((6,)), dma((6,)), dma((6,)),
        dma((3,)),
    ]
    return pl.pallas_call(
        functools.partial(kernel, cut),
        out_shape=jax.ShapeDtypeStruct((T, R, 2 * HALF), BF),
        in_specs=[pl.BlockSpec(memory_space=pltpu.SMEM), hbm, hbm, hbm, vm, vm],
        out_specs=pl.BlockSpec(memory_space=pl.ANY),
        scratch_shapes=scratch,
        compiler_params=pltpu.CompilerParams(
            collective_id=cut, has_side_effects=True, vmem_limit_bytes=60 << 20
        ),
        name="attend_%d" % cut,
    )(lengths, q, k, v, q_gain, k_gain)


def per_device(q_in, k_in, v_in, q_gain, k_gain, lengths):
    args = (
        lengths,
        jnp.transpose(q_in, (1, 0, 2)),
        jnp.transpose(k_in, (1, 0, 2)),
        jnp.transpose(v_in, (1, 0, 2)),
        q_gain,
        k_gain,
    )
    fits = jnp.sum((lengths > REACH).astype(jnp.int32)) <= CUT
    res = lax.cond(
        fits,
        functools.partial(run, CUT),
        functools.partial(run, R),
        *args,
    )
    return jnp.transpose(res, (1, 0, 2))


def solution(mesh):
    placed = P(None, ("grp", "uly", "blk"), None)
    return jax.shard_map(
        per_device,
        mesh=mesh,
        in_specs=(placed, placed, placed, P(), P(), P()),
        out_specs=placed,
        check_vma=False,
    )
```

```python
import functools
import math

import jax
import jax.numpy as jnp
from jax import lax
from jax.experimental import pallas as pl
from jax.experimental.pallas import tpu as pltpu
from jax.sharding import PartitionSpec as P

HD = 128
T = 12
R = 16
HALF = 1280
SLOTS = 64
KEYS = 3072
TILE = 384
BLOCK = 768
SUB = 256
REACH = 1536
CUT = 10
LOG2E = math.log2(math.e)
MESH = pl.DeviceIdType.MESH
BF = jnp.bfloat16
F32 = jnp.float32


def slot_pos(shape, slot, zpar):
    w = lax.broadcasted_iota(jnp.int32, shape, 1)
    cc = (w >= T).astype(jnp.int32)
    t = w - T * cc
    x = slot & 3
    zh = (slot >> 2) & 3
    yh = (slot >> 4) & 1
    yl = slot >> 5
    z = zh * 2 + zpar
    return ((((yl * 2 + cc) * 4 + x) * 2 + yh) * 8 + z) * T + t


def group_rank(yh, z):
    k = (z >> 1) + (z & 1) * (4 + 2 * (1 - ((z >> 1) & 1)) - (z >> 1) + (z >> 2))
    return jnp.where((k & 1) == yh, k, 15 - k)


def rank_group(k):
    j = k if k < 8 else 15 - k
    z = 2 * j if j < 4 else (3, 7, 1, 5)[j - 4]
    yh = (j & 1) if k < 8 else 1 - (j & 1)
    return yh * 8 + z


def kernel(
    cut,
    len_hbm, q_ref, k_ref, v_ref, qg_ref, kg_ref, out_ref,
    len_ref, raw, halves, own_v, mates, perm, sb, ss, rel, rels, rb, rsh, rm, rmsh, ka, va, scr,
    obs, oshs, ob, osh, fin,
    ex_s, ex_r, main_s, main_r, fwd_s, fwd_r, sh_s, sh_r, fsh_s, fsh_r,
    rel_s, rel_r, rels_s, rels_r, o_s, o_r, osh_s, osh_r, fin_s, fin_r, fin_l, in_s,
):
    g = lax.axis_index("grp")
    x = lax.axis_index("uly")
    blk = lax.axis_index("blk")
    c = blk & 1
    yl = blk >> 1
    z = g & 7
    yh = g >> 3
    zp = z & 1
    zh = z >> 1
    slot = ((yl * 2 + yh) * 4 + zh) * 4 + x
    sgrp = slot >> 4
    xhalf = x >> 1
    xl_me = x & 1
    rank_me = group_rank(yh, z)
    short = rank_me >= cut
    three = yl == (zp ^ xl_me)
    mate = (g, x, yl * 2 + 1 - c)
    next_chip = (g, x, (1 - yl) * 2 + c)
    own = jnp.logical_and(xhalf == c, zp == c)

    def far_first(i):
        j = i & 7
        return (z + jnp.where((j & 1) == 0, 4 + (j >> 1), 3 - (j >> 1))) & 7

    def dest(i):
        y2 = yl ^ (i & 1)
        xl = (i >> 1) & 1
        ty = yh ^ ((i >> 2) & 1)
        tz = far_first(i >> 3)
        return group_rank(ty, tz), xl, y2, ((ty << 3) | tz, 2 * c + xl, y2 * 2 + zp)

    def is_self(i):
        return jnp.logical_and(own, i == 2 * xl_me + 56)

    def source(s):
        return (
            (((s >> 4) & 1) << 3) | (((s >> 2) & 3) << 1) | c,
            s & 3,
            ((s >> 5) << 1) | xhalf,
        )

    def remote(src, dst, ssem, rsem, to):
        return pltpu.make_async_remote_copy(
            src_ref=src, dst_ref=dst, send_sem=ssem, recv_sem=rsem,
            device_id=to, device_id_type=MESH,
        )

    def send(src, dst, ssem, rsem, to, here):
        @pl.when(here)
        def _():
            pltpu.make_async_copy(src, dst, rsem).start()

        @pl.when(jnp.logical_not(here))
        def _():
            remote(src, dst, ssem, rsem, to).start()

    def wait_for(ref, sem):
        pltpu.make_async_copy(ref, ref, sem).wait()

    mine_cols = pl.ds(pl.multiple_of(c * HALF, HALF), HALF)
    mate_cols = pl.ds(pl.multiple_of((1 - c) * HALF, HALF), HALF)
    loads = [
        pltpu.make_async_copy(q_ref, raw.at[0], in_s.at[0]),
        pltpu.make_async_copy(k_ref, raw.at[1], in_s.at[1]),
        pltpu.make_async_copy(v_ref.at[:, :, mine_cols], own_v, in_s.at[2]),
        pltpu.make_async_copy(len_hbm, len_ref, in_s.at[3]),
    ]
    for load in loads:
        load.start()

    barrier = pltpu.get_barrier_semaphore()

    def greet(i, carry):
        @pl.when(jnp.logical_not(is_self(i)))
        def _():
            pl.semaphore_signal(barrier, inc=1, device_id=dest(i)[3], device_id_type=MESH)

        @pl.when(jnp.logical_not(jnp.logical_and(own, i == slot)))
        def _():
            pl.semaphore_signal(barrier, inc=1, device_id=source(i), device_id_type=MESH)

        return carry

    lax.fori_loop(0, SLOTS, greet, 0)
    pl.semaphore_signal(barrier, inc=1, device_id=mate, device_id_type=MESH)
    pl.semaphore_signal(barrier, inc=1, device_id=next_chip, device_id_type=MESH)

    loads[3].wait()
    sizes = [len_ref[i] for i in range(R)]
    ranks = []
    count = jnp.int32(0)
    for i in range(R):
        rank = jnp.int32(0)
        for j in range(R):
            if j != i:
                ahead = sizes[j] >= sizes[i] if j < i else sizes[j] > sizes[i]
                rank = rank + ahead.astype(jnp.int32)
        ranks.append(rank)
        count = count + jnp.where(rank == rank_me, sizes[i], 0)

    def norm_into(gain_ref, at):
        gain = gain_ref[...][None, :]
        for t in range(T):
            wide = raw[at, t].astype(F32)
            power = jnp.mean(wide * wide, axis=-1, keepdims=True)
            y = (wide * lax.rsqrt(power + 1e-06) * gain).astype(BF)
            halves[0, at, t] = y[:, :HALF]
            halves[1, at, t] = y[:, HALF:]

    loads[0].wait()
    norm_into(qg_ref, 0)

    @pl.when(own)
    def _():
        pl.semaphore_wait(barrier, 2 * SLOTS)

    @pl.when(jnp.logical_not(own))
    def _():
        pl.semaphore_wait(barrier, 2 * SLOTS + 2)

    exch = [
        remote(halves.at[1 - c, 0], mates.at[0], ex_s.at[0], ex_r.at[0], mate),
        remote(halves.at[1 - c, 1], mates.at[1], ex_s.at[1], ex_r.at[1], mate),
        remote(v_ref.at[:, :, mate_cols], mates.at[2], ex_s.at[2], ex_r.at[2], mate),
    ]
    exch[2].start()
    exch[0].start()
    loads[1].wait()
    norm_into(kg_ref, 1)
    exch[1].start()

    shape = (R, 2 * T, TILE)
    ow = lax.broadcasted_iota(jnp.int32, shape, 1)
    occ = (ow >= T).astype(jnp.int32)
    col = lax.broadcasted_iota(jnp.int32, (1, 1, TILE), 2)
    rank_of = jnp.zeros((1, 1, TILE), jnp.int32)
    for i in range(R):
        rank_of = jnp.where((col & 15) == i, ranks[i], rank_of)
    place_of = (col >> 4) + 64 * rank_of
    want = jnp.where(occ == c, 0, 1) * T + ow - T * occ
    want = want + 64 * lax.broadcasted_iota(jnp.int32, shape, 0)
    perm[...] = (want == place_of).astype(F32).reshape(TILE, TILE).astype(BF)

    loads[2].wait()
    for at in range(3):
        exch[at].wait()

    def pack(at, xl, first, width):
        cols = slice(xl * 640 + first * HD, xl * 640 + (first + width) * HD)
        mine = own_v[:, :, cols] if at == 2 else halves[c, at, :, :, cols]
        mine = mine.reshape(T * R, width * HD)
        theirs = mates[at, :, :, cols].reshape(T * R, width * HD)
        both = jnp.concatenate([mine, theirs], axis=0)
        res = jnp.dot(perm[...], both, preferred_element_type=F32)
        return res.reshape(R, 2 * T, width * HD)

    parts = ((0, 4, 0), (4, 12, 1), (12, 16, 0))

    for at in range(3):
        for xl in range(2):
            for hp in range(2):
                res = pack(at, xl, 3 * hp, 2)
                two = jnp.concatenate([res[:, :, :HD], res[:, :, HD:]], axis=1).astype(BF)
                for lo, hi, odd in parts:
                    sb[lo:hi, xl, hp ^ odd ^ xl, at * 48 : at * 48 + 48, :] = two[lo:hi]

    far_ranks = R - cut
    if far_ranks:
        @pl.when(yl == 0)
        def _():
            remote(sb.at[pl.ds(cut, far_ranks), :, 1], rel, rel_s, rel_r, next_chip).start()

    def send_main(i, carry):
        k, xl, y2, to = dest(i)
        ok = jnp.logical_or(k < cut, jnp.logical_and(yl == 0, y2 == 0))

        @pl.when(ok)
        def _():
            send(sb.at[k, xl, y2], rb.at[slot], main_s, main_r.at[sgrp], to, is_self(i))

        return carry

    lax.fori_loop(0, SLOTS, send_main, 0)

    for xl in range(2):
        kv = jnp.concatenate([pack(1, xl, 2, 1), pack(2, xl, 2, 1)], axis=1)
        ss[:, xl, 0:48, :] = kv.astype(BF)
        qq = jnp.concatenate([pack(0, xl, 2, 1), jnp.zeros((R, 8, HD), F32)], axis=1)
        ss[:, xl, 48:80, :] = qq.astype(BF)

    def pass_on(k, xl, src, dst, ssem, rsem):
        gk = rank_group(k)
        here = jnp.logical_and(own, jnp.logical_and(g == gk, xl_me == xl))
        send(src, dst, ssem, rsem, (gk, 2 * c + xl, 2 + zp), here)

    def spare(k):
        return 1 ^ (rank_group(k) & 1)

    if far_ranks:
        @pl.when(yl == 0)
        def _():
            for k in range(cut, R):
                at = k - cut
                remote(
                    ss.at[k, spare(k)], rels.at[at], rels_s.at[at], rels_r.at[at], next_chip
                ).start()

        @pl.when(yl == 1)
        def _():
            wait_for(rel, rel_r)
            for k in range(cut, R):
                for xl in range(2):
                    pass_on(
                        k, xl, rel.at[k - cut, xl], rb.at[slot & 31], main_s, main_r.at[yh]
                    )

    def send_shared(i, carry):
        xl = i & 1
        ty = yh ^ ((i >> 1) & 1)
        tz = far_first(i >> 2)
        k = group_rank(ty, tz)
        y2 = (tz & 1) ^ xl
        ok = jnp.logical_or(k < cut, jnp.logical_and(yl == 0, y2 == 0))
        here = jnp.logical_and(jnp.logical_and(own, three), i == xl_me + 28)

        @pl.when(ok)
        def _():
            send(
                ss.at[k, xl], rsh.at[slot], sh_s, sh_r.at[sgrp],
                ((ty << 3) | tz, 2 * c + xl, y2 * 2 + zp), here,
            )

        return carry

    lax.fori_loop(0, SLOTS // 2, send_shared, 0)

    if far_ranks:
        @pl.when(yl == 1)
        def _():
            for k in range(cut, R):
                at = k - cut
                wait_for(rels.at[at], rels_r.at[at])
                pass_on(k, spare(k), rels.at[at], rsh.at[slot & 31], sh_s, sh_r.at[yh])

    lane0 = (lax.broadcasted_iota(jnp.int32, (SUB, HD), 1) == 0).astype(F32).astype(BF)

    def live_rows(slots, first, zpar):
        s = lax.broadcasted_iota(jnp.int32, (slots, 2 * T, HD), 0) + first
        flag = slot_pos((slots, 2 * T, HD), s, zpar) < count
        return flag.astype(F32).reshape(slots * 2 * T, HD)

    def masks(i, carry):
        flag = live_rows(16, (i & 3) * 16, jnp.where(i < 4, c, 1 - c))
        rows = pl.ds(pl.multiple_of(i * TILE, TILE), TILE)
        for h in range(3):
            ka[h, rows, HD:] = ((flag - 1.0) * 1e30).astype(BF)
            va[h, rows, HD:] = jnp.ones((TILE, HD), BF)
        return carry

    lax.fori_loop(0, 8, masks, 0)

    def place(ref, h, rows, value):
        ref[h, rows, :HD] = value.reshape(TILE, HD).astype(BF)

    def gather(some, arrived, forward, ours, theirs, heads):
        def lay(i, value):
            rows = slice(i * TILE, (i + 1) * TILE)
            kv = value.astype(F32)
            for n, h in enumerate(heads):
                place(ka, h, rows, kv[:, 24 * n : 24 * n + 24])
                m = n + len(heads)
                place(va, h, rows, kv[:, 24 * m : 24 * m + 24])

        def blank(i):
            rows = slice(i * TILE, (i + 1) * TILE)
            for h in heads:
                ka[h, rows, :HD] = jnp.zeros((TILE, HD), BF)
                va[h, rows, :HD] = jnp.zeros((TILE, HD), BF)

        def first(i):
            arrived(i)
            forward(i).start()
            lay(i, ours(i))

        def second(i):
            forward(i).wait()
            lay(4 + i, theirs(i))

        for step, shift in ((first, 0), (second, 4)):
            for i in range(4):
                if i < 2 or not some:
                    step(i)
                else:
                    @pl.when(short)
                    def _(i=i, shift=shift):
                        blank(shift + i)

                    @pl.when(jnp.logical_not(short))
                    def _(i=i, step=step):
                        step(i)

    def grp(i):
        return pl.ds(16 * i, 16)

    gather(
        far_ranks,
        lambda i: wait_for(rb.at[grp(i)], main_r.at[i]),
        lambda i: remote(
            rb.at[grp(i), pl.ds(48, 96)], rm.at[grp(i)], fwd_s.at[i], fwd_r.at[i], mate
        ),
        lambda i: rb[16 * i : 16 * i + 16, 48:144, :],
        lambda i: rm[16 * i : 16 * i + 16],
        (0, 1),
    )

    scale = HD ** (-0.5) * LOG2E

    def attend(q, h, live):
        step = 512
        outs = []
        for n in range(BLOCK // SUB):
            rows = slice(n * SUB, (n + 1) * SUB)
            qa = jnp.concatenate([q[rows], lane0], axis=1)
            top = None
            for j in range(KEYS // step):
                cols = slice(j * step, (j + 1) * step)
                part = lax.dot_general(
                    qa, ka[h, cols, :], (((1,), (1,)), ((), ())),
                    preferred_element_type=F32,
                )
                scr[rows, cols] = part
                for i in range(step // HD):
                    piece = part[:, i * HD : (i + 1) * HD]
                    top = piece if top is None else jnp.maximum(top, piece)
            peak = jnp.max(top, axis=1, keepdims=True)
            mixed = None
            for j in range(KEYS // step):
                cols = slice(j * step, (j + 1) * step)
                weights = jnp.exp2((scr[rows, cols] - peak) * scale).astype(BF)
                part = jnp.dot(weights, va[h, cols, :], preferred_element_type=F32)
                mixed = part if mixed is None else mixed + part
            outs.append(jnp.where(live[rows] > 0.0, mixed[:, :HD] / mixed[:, HD:], 0.0))
        return jnp.concatenate(outs, axis=0)

    passes = jnp.where(short, 1, 2)

    def back_from(ref, to, ssem, rsem, first):
        def back(j, carry):
            s = first + (j ^ (slot & 31))
            here = jnp.logical_and(own, s == slot)
            send(ref.at[s], to, ssem, rsem, source(s), here)
            return carry

        lax.fori_loop(0, 32, back, 0)

    def main_pass(i, carry):
        at = pl.ds(pl.multiple_of(i * 32, 32), 32)
        live = live_rows(32, i * 32, c)
        qq = rb[at, 0:48, :].astype(F32)
        res = []
        for h in range(2):
            q = qq[:, 24 * h : 24 * h + 24].reshape(BLOCK, HD).astype(BF)
            res.append(attend(q, h, live).reshape(32, 2 * T, HD))
        obs[at] = jnp.concatenate(res, axis=1).astype(BF)
        rsem = o_r.at[xl_me, short.astype(jnp.int32)]
        back_from(obs, ob.at[rank_me, xl_me, yl], o_s, rsem, i * 32)
        return carry

    lax.fori_loop(0, passes, main_pass, 0)

    def third_pass(i, carry):
        at = pl.ds(pl.multiple_of(i * 32, 32), 32)
        live = live_rows(32, i * 32, c)
        q = rsh[at, 48:80, :].astype(F32)[:, 0:24].reshape(BLOCK, HD).astype(BF)
        res = attend(q, 2, live).reshape(32, 2 * T, HD)
        oshs[at] = jnp.concatenate([res, jnp.zeros((32, 8, HD), F32)], axis=1).astype(BF)
        rsem = osh_r.at[xl_me, short.astype(jnp.int32)]
        back_from(oshs, osh.at[rank_me, xl_me], osh_s, rsem, i * 32)
        return carry

    def sent_back(ref, sem):
        whole = jnp.logical_not(short)
        one = jnp.logical_and(own, jnp.logical_or(whole, yl == 0))
        for n, kind in ((SLOTS, whole), (SLOTS // 2, short)):
            if n == SLOTS or far_ranks:
                @pl.when(jnp.logical_and(kind, one))
                def _(n=n):
                    wait_for(ref.at[pl.ds(0, n - 1)], sem)

                @pl.when(jnp.logical_and(kind, jnp.logical_not(one)))
                def _(n=n):
                    wait_for(ref.at[pl.ds(0, n)], sem)

    @pl.when(three)
    def _():
        gather(
            far_ranks,
            lambda i: wait_for(rsh.at[grp(i)], sh_r.at[i]),
            lambda i: remote(
                rsh.at[grp(i), pl.ds(0, 48)], rmsh.at[grp(i)], fsh_s.at[i], fsh_r.at[i], mate
            ),
            lambda i: rsh[16 * i : 16 * i + 16, 0:48, :],
            lambda i: rmsh[16 * i : 16 * i + 16],
            (2,),
        )
        lax.fori_loop(0, passes, third_pass, 0)

    def unpack(value):
        res = lax.dot_general(
            perm[...], value, (((0,), (0,)), ((), ())), preferred_element_type=F32
        )
        return res.astype(BF)

    def store(res, xl, first, width):
        cols = slice(xl * 640 + first * HD, xl * 640 + (first + width) * HD)
        fin[0, :, :, cols] = res[: T * R].reshape(T, R, width * HD)
        fin[1, :, :, cols] = res[T * R :].reshape(T, R, width * HD)

    def returned(ref, sem, xl):
        wait_for(ref.at[pl.ds(0, cut), xl], sem.at[xl, 0])
        if far_ranks:
            @pl.when(yl == 0)
            def _():
                wait_for(ref.at[pl.ds(cut, far_ranks), xl], sem.at[xl, 1])

            @pl.when(yl == 1)
            def _():
                ref[cut:, xl] = jnp.zeros(ref[cut:, xl].shape, BF)

    done = []

    def ship(first, width):
        n = len(done)
        at = pl.ds(pl.multiple_of(c * HALF + first, HD), width)
        here = pl.ds(first, width)
        far = remote(
            fin.at[1, :, :, here], out_ref.at[:, :, at], fin_s.at[n], fin_r.at[n], mate
        )
        far.start()
        near = pltpu.make_async_copy(fin.at[0, :, :, here], out_ref.at[:, :, at], fin_l.at[n])
        near.start()
        done.append((far, near))

    for xl in range(2):
        returned(ob, o_r, xl)
        for hp in range(2):
            got = jnp.concatenate(
                [ob[lo:hi, xl, hp ^ odd ^ xl] for lo, hi, odd in parts], axis=0
            ).astype(F32)
            flat = [got[:, 24 * h : 24 * h + 24].reshape(TILE, HD) for h in range(2)]
            store(unpack(jnp.concatenate(flat, axis=1).astype(BF)), xl, 3 * hp, 2)
            ship(xl * 640 + 384 * hp, 256)
    for xl in range(2):
        returned(osh, osh_r, xl)
        got = osh[:, xl].astype(F32)[:, 0:24].reshape(TILE, HD)
        store(unpack(got.astype(BF)), xl, 2, 1)
        ship(xl * 640 + 256, 128)
    for far, near in done:
        far.wait()
        near.wait()

    sent_back(obs, o_s)

    @pl.when(three)
    def _():
        sent_back(oshs, osh_s)

    n_main = SLOTS - 2 * far_ranks
    n_shared = SLOTS // 2 - far_ranks

    def sent(ref, n, sem, one):
        @pl.when(one)
        def _():
            wait_for(ref.at[pl.ds(0, n - 1)], sem)

        @pl.when(jnp.logical_not(one))
        def _():
            wait_for(ref.at[pl.ds(0, n)], sem)

    sent(rb, n_main, main_s, own)
    sent(rsh, n_shared, sh_s, jnp.logical_and(own, three))
    if far_ranks:
        @pl.when(yl == 0)
        def _():
            wait_for(rel, rel_s)
            for at in range(far_ranks):
                wait_for(rels.at[at], rels_s.at[at])


def run(cut, lengths, q, k, v, q_gain, k_gain):
    vm = pl.BlockSpec(memory_space=pltpu.VMEM)
    hbm = pl.BlockSpec(memory_space=pl.ANY)
    dma = pltpu.SemaphoreType.DMA
    far = max(R - cut, 1)
    scratch = [
        pltpu.SMEM((R,), jnp.int32),
        pltpu.VMEM((2, T, R, 2 * HALF), BF),
        pltpu.VMEM((2, 2, T, R, HALF), BF),
        pltpu.VMEM((T, R, HALF), BF),
        pltpu.VMEM((3, T, R, HALF), BF),
        pltpu.VMEM((TILE, TILE), BF),
        pltpu.VMEM((R, 2, 2, 144, HD), BF),
        pltpu.VMEM((R, 2, 80, HD), BF),
        pltpu.VMEM((far, 2, 144, HD), BF),
        pltpu.VMEM((far, 80, HD), BF),
        pltpu.VMEM((SLOTS, 144, HD), BF),
        pltpu.VMEM((SLOTS, 80, HD), BF),
        pltpu.VMEM((SLOTS, 96, HD), BF),
        pltpu.VMEM((SLOTS, 48, HD), BF),
        pltpu.VMEM((3, KEYS, 2 * HD), BF),
        pltpu.VMEM((3, KEYS, 2 * HD), BF),
        pltpu.VMEM((BLOCK, KEYS), F32),
        pltpu.VMEM((SLOTS, 48, HD), BF),
        pltpu.VMEM((SLOTS, 32, HD), BF),
        pltpu.VMEM((R, 2, 2, 48, HD), BF),
        pltpu.VMEM((R, 2, 32, HD), BF),
        pltpu.VMEM((2, T, R, HALF), BF),
        dma((3,)), dma((3,)),
        dma, dma((4,)),
        dma((4,)), dma((4,)),
        dma, dma((4,)),
        dma((4,)), dma((4,)),
        dma, dma, dma((far,)), dma((far,)),
        dma, dma((2, 2)),
        dma, dma((2, 2)),
        dma((6,)), dma((6,)), dma((6,)),
        dma((4,)),
    ]
    return pl.pallas_call(
        functools.partial(kernel, cut),
        out_shape=jax.ShapeDtypeStruct((T, R, 2 * HALF), BF),
        in_specs=[hbm, hbm, hbm, hbm, vm, vm],
        out_specs=pl.BlockSpec(memory_space=pl.ANY),
        scratch_shapes=scratch,
        compiler_params=pltpu.CompilerParams(
            collective_id=cut, has_side_effects=True, vmem_limit_bytes=60 << 20
        ),
        name="attend_%d" % cut,
    )(lengths, q, k, v, q_gain, k_gain)


def per_device(q_in, k_in, v_in, q_gain, k_gain, lengths):
    args = (
        lengths,
        jnp.transpose(q_in, (1, 0, 2)),
        jnp.transpose(k_in, (1, 0, 2)),
        jnp.transpose(v_in, (1, 0, 2)),
        q_gain,
        k_gain,
    )
    fits = jnp.sum((lengths > REACH).astype(jnp.int32)) <= CUT
    res = lax.cond(
        fits,
        functools.partial(run, CUT),
        functools.partial(run, R),
        *args,
    )
    return jnp.transpose(res, (1, 0, 2))


def solution(mesh):
    placed = P(None, ("grp", "uly", "blk"), None)
    return jax.shard_map(
        per_device,
        mesh=mesh,
        in_specs=(placed, placed, placed, P(), P(), P()),
        out_specs=placed,
        check_vma=False,
    )
```
